128 devices in a mesh: seqa: 16 (over x, z_hi, core), seqb: 8 (over y, z_lo).
Axes of the slice: x: 4, y: 4, z: 4 (z_hi: 2, z_lo: 2; z = z_hi * 2 + z_lo), core: 2. Of those that a mesh axis runs over, the one named last changes fastest.
Arguments:
- queries: bfloat16 [131072, 1024], P(('seqa', 'seqb')), may hold values from -6 to 6
- keys: bfloat16 [131072, 1024], P(('seqa', 'seqb')), may hold values from -6 to 6
- values: bfloat16 [131072, 1024], P(('seqa', 'seqb')), may hold values from -6 to 6
- grad_out: bfloat16 [131072, 1024], P(('seqa', 'seqb')), may hold values from -6 to 6
Outputs:
- attended: bfloat16 [131072, 1024], P(('seqa', 'seqb'))
- grad_queries: bfloat16 [131072, 1024], P(('seqa', 'seqb'))
- grad_keys: bfloat16 [131072, 1024], P(('seqa', 'seqb'))
- grad_values: bfloat16 [131072, 1024], P(('seqa', 'seqb'))
The draws below stay inside these ranges and needn't reach their ends.
All inputs are finite; a program needn't handle non-finite values.
Results may differ from the reference program's by a relative error of at most 0.03.
Values may be sent and summed in bfloat16 or wider, within the bound.
No kernel may reach another device: no remote copies, remote signals or barrier semaphores. Data moves between devices by JAX's collectives and lax.ppermute only.
A program may use at most 256 MiB of HBM per device.

```python
import math
import jax
import jax.numpy as jnp
from jax import lax

HEADS = 16
HEAD_DIM = 64
BLOCK = 256
LEVELS = 3
D = 1024
SEQ = 131072


def draw_queries(key, part):
    own_key = jax.random.fold_in(key, 3)
    drawn = jax.random.truncated_normal(own_key, -6.0, 6.0, (SEQ, D), jnp.float32)
    return drawn.astype(jnp.bfloat16)


def draw_keys(key, part):
    own_key = jax.random.fold_in(key, 5)
    drawn = jax.random.truncated_normal(own_key, -6.0, 6.0, (SEQ, D), jnp.float32)
    return drawn.astype(jnp.bfloat16)


def steps_of(key, dims, shards, low, largest):
    factor_of = 1.0
    for axis_at, parts in shards:
        steps = jax.random.uniform(jax.random.fold_in(jax.random.fold_in(key, 6), axis_at), (parts,), jnp.float32, low / len(shards), largest / len(shards))
        factor_of = factor_of * jnp.repeat(jnp.exp(steps), dims[axis_at] // parts).reshape((-1,) + (1,) * (len(dims) - 1 - axis_at))
    return factor_of


def bell_draw(key, shape, spread, limit, cuts=(), held_as=jnp.bfloat16):
    values = spread * jax.random.normal(key, shape, jnp.float32)
    if cuts:
        values = values * steps_of(key, shape, cuts, -0.22, 0.18)
    return jnp.clip(values, -limit, limit).astype(held_as)


def setup_inputs(seed: int = 0) -> dict:
    arg_keys = jax.random.split(jax.random.key(seed), 5)
    return {
        "queries": draw_queries(jax.random.fold_in(arg_keys[4], 71), 0),
        "keys": draw_keys(jax.random.fold_in(arg_keys[4], 71), 0),
        "values": bell_draw(arg_keys[2], (SEQ, D), 1.0, 6.0, ((0, 128),)),
        "grad_out": bell_draw(arg_keys[3], (SEQ, D), 1.0, 6.0, ((0, 128),)),
    }


LOG_TWO = math.log(2.0)


def coarsen(pieces, stride):
    if stride == 1:
        return pieces
    shaped = pieces.astype(jnp.float32).reshape(pieces.shape[0] // stride, stride, pieces.shape[1])
    return shaped.mean(axis=1).astype(jnp.bfloat16)


def inside(row_index, bound_value):
    return (row_index >= 0) & (row_index < bound_value)


def attend_block(query_rows, grad_rows, key_rows, value_rows, bias_rows, usable):
    factor = HEAD_DIM ** -0.5
    exact = lax.Precision.HIGHEST
    query_part = query_rows.astype(jnp.float32).reshape(BLOCK, HEADS, HEAD_DIM)
    grad_part = grad_rows.astype(jnp.float32).reshape(BLOCK, HEADS, HEAD_DIM)
    key_part = key_rows.astype(jnp.float32).reshape(-1, HEADS, HEAD_DIM)
    value_part = value_rows.astype(jnp.float32).reshape(-1, HEADS, HEAD_DIM)
    scores = jnp.einsum("qhd,khd->hqk", query_part, key_part, precision=exact) * factor + bias_rows
    scores = jnp.where(usable, scores, -jnp.inf)
    highest = jnp.max(scores, axis=2, keepdims=True)
    weights = jnp.exp(scores - highest)
    probability = weights / jnp.sum(weights, axis=2, keepdims=True)
    probs_low = probability.astype(jnp.bfloat16).astype(jnp.float32)
    mixed_rows = jnp.einsum("hqk,khd->qhd", probs_low, value_part, precision=exact).astype(jnp.bfloat16)
    inner_sum = jnp.sum(grad_part * mixed_rows.astype(jnp.float32), axis=2).T[:, :, None]
    dprobs = jnp.einsum("qhd,khd->hqk", grad_part, value_part, precision=exact)
    dscores = (probability * (dprobs - inner_sum)).astype(jnp.bfloat16).astype(jnp.float32)
    query_grad = jnp.einsum("hqk,khd->qhd", dscores, key_part, precision=exact) * factor
    key_grad = jnp.einsum("hqk,qhd->khd", dscores, query_part, precision=exact) * factor
    value_grad = jnp.einsum("hqk,qhd->khd", probs_low, grad_part, precision=exact)
    return mixed_rows, query_grad, key_grad, value_grad


def reference(queries, keys, values, grad_out):
    pieces = jnp.concatenate([keys, values], axis=1)
    features = queries.shape[1]
    breadth = 2 * features
    blocks = SEQ // BLOCK
    half_size = BLOCK // 2
    edge_zeros = jnp.zeros((BLOCK, breadth), jnp.bfloat16)
    padded = [jnp.concatenate([edge_zeros, pieces, edge_zeros], axis=0)]
    for level_number in range(1, LEVELS + 1):
        margin = jnp.zeros((3 * half_size, breadth), jnp.bfloat16)
        padded.append(jnp.concatenate([margin, coarsen(pieces, 2 ** level_number), margin], axis=0))
    bias_rows = jnp.concatenate([jnp.zeros((3 * BLOCK,), jnp.float32)] + [jnp.full((3 * half_size,), level_number * LOG_TWO, jnp.float32) for level_number in range(1, LEVELS + 1)])

    def placements(block_index):
        placed = []
        for offset in (-1, 0, 1):
            source = block_index + offset
            placed.append((0, ((source + 1) * BLOCK).astype(jnp.int32), BLOCK, inside(source, blocks)))
        for level_number in range(1, LEVELS + 1):
            span_number = block_index // 2 ** (level_number - 1)
            odd_span = span_number % 2 == 1
            for even_step, odd_step in ((-2, -3), (2, -2), (3, 2)):
                source = span_number + jnp.where(odd_span, odd_step, even_step).astype(jnp.int32)
                placed.append((level_number, ((source + 3) * half_size).astype(jnp.int32), half_size,
                               inside(source, blocks // 2 ** (level_number - 1))))
        return placed

    def block_step(carried, block_index):
        placed = placements(block_index)
        window = jnp.concatenate([lax.dynamic_slice_in_dim(padded[level_number], start, height, 0)
                                  for level_number, start, height, validity in placed], axis=0)
        usable = jnp.concatenate([jnp.broadcast_to(validity, (height,)) for level_number, start, height, validity in placed])
        first = (block_index * BLOCK).astype(jnp.int32)
        query_rows = lax.dynamic_slice_in_dim(queries, first, BLOCK, 0)
        grad_rows = lax.dynamic_slice_in_dim(grad_out, first, BLOCK, 0)
        mixed_rows, query_grad, key_grad, value_grad = attend_block(query_rows, grad_rows, window[:, :features], window[:, features:], bias_rows, usable)
        window_grads = jnp.concatenate([key_grad.reshape(-1, features), value_grad.reshape(-1, features)], axis=1)
        updated = list(carried)
        offset = 0
        for level_number, start, height, validity in placed:
            portion = window_grads[offset:offset + height]
            current = lax.dynamic_slice_in_dim(updated[level_number], start, height, 0)
            updated[level_number] = lax.dynamic_update_slice_in_dim(updated[level_number], current + portion, start, 0)
            offset += height
        return tuple(updated), (mixed_rows.reshape(BLOCK, features), query_grad.reshape(BLOCK, features).astype(jnp.bfloat16))

    initial = [jnp.zeros((SEQ + 2 * BLOCK, breadth), jnp.float32)]
    for level_number in range(1, LEVELS + 1):
        initial.append(jnp.zeros((SEQ // 2 ** level_number + 6 * half_size, breadth), jnp.float32))
    carried, (mixed_all, query_all) = lax.scan(block_step, tuple(initial), jnp.arange(blocks, dtype=jnp.int32))
    summed = carried[0][BLOCK:-BLOCK]
    for level_number in range(1, LEVELS + 1):
        stride = 2 ** level_number
        owned = carried[level_number][3 * half_size:-3 * half_size]
        summed = summed + jnp.repeat(owned / stride, stride, axis=0)
    return (mixed_all.reshape(SEQ, features), query_all.reshape(SEQ, features),
            summed[:, :features].astype(jnp.bfloat16), summed[:, features:].astype(jnp.bfloat16))
```

```python
import math

import jax
import jax.numpy as jnp
from jax import lax
from jax.experimental import pallas as pl
from jax.experimental.pallas import tpu as pltpu
from jax.sharding import PartitionSpec as P

HEAD_DIM = 64
BLOCK = 256
HALF = 128
PAIR = 128
AXES = ("seqa", "seqb")
GROUPS = (2, 2, 2, 2)
LOG2E = math.log2(math.e)
BF16 = jnp.bfloat16
F32 = jnp.float32
NT = (((1,), (1,)), ((), ()))
NN = (((1,), (0,)), ((), ()))

BASE = (0, 1536, 2560, 3072)
ROWS = 3456

TILES = (
    (0, 0, 256, 1024, 0, 1),
    (0, 256, 256, 512, 0, 2),
    (0, 512, 256, 0, 0, 3),
    (0, 768, 256, 0, 1, 3),
    (0, 1024, 256, 0, 2, 2),
    (0, 1280, 256, 0, 3, 1),
    (1, 0, 128, 512, 1, 1),
    (1, 128, 256, 0, 0, 2),
    (1, 384, 128, 0, 0, 1),
    (1, 512, 128, 512, 3, 1),
    (1, 640, 256, 0, 2, 2),
    (1, 896, 128, 0, 2, 1),
    (2, 0, 128, 0, 0, 2),
    (2, 128, 256, 0, 0, 4),
    (2, 384, 128, 1024, 2, 2),
    (3, 0, 384, 0, 0, 4),
)


def pieces(b, h):
    at = h * 256
    low = (b // 2) * 512 + (1 - b % 2) * 128
    return (
        (0, b * 256, 256, 1024 + at),
        (0, b * 256 + 256, 256, 512 + at),
        (0, b * 256 + 512, 256, at),
        (1, low, 384, (b % 2) * 512 + at),
        (2, (b // 2) * 128, 384, b * 512 + at),
        (3, 0, 384, b * 512 + at),
    )


def dot(a, b, dims=NN):
    return lax.dot_general(a, b, dims, preferred_element_type=F32)


def mean_rows(ref, start, count, stride):
    total = ref[pl.ds(start, count, stride=stride), :]
    for i in range(1, stride):
        total = total + ref[pl.ds(start + i, count, stride=stride), :]
    return total * (1.0 / stride)


def spread_rows(ref, start, rows, stride):
    for i in range(stride):
        at = pl.ds(start + i, rows.shape[0], stride=stride)
        ref[at, :] = ref[at, :] + rows


def attend_kernel(
    valid, q, k, v, do, lk, lv, uk, uv, fk, fv,
    o, dq, gk, gv, glk, glv, guk, guv, gfk, gfv,
    kext, vext, kt, vt, e0, e1, e2, e3, x0, x1, x2, x3,
    qz, doz, qs, dos, inn, rls, ftmp, gtmp, flag,
):
    es = (e0, e1, e2, e3)
    xs = (x0, x1, x2, x3)
    lane = lax.broadcasted_iota(jnp.int32, (256, PAIR), 1)
    first = lane < HEAD_DIM

    for own, low, up, far, ext in ((k, lk, uk, fk, kext), (v, lv, uv, fv, vext)):
        ext[0:256] = low[0:256]
        ext[256:1280] = own[...]
        ext[1280:1536] = up[0:256]
        ftmp[0:1024] = own[...].astype(F32)
        spans = mean_rows(ftmp, 0, 512, 2).astype(BF16)
        b1 = BASE[1]
        ext[b1 + 256 : b1 + 384] = spans[384:512]
        ext[b1 + 384 : b1 + 512] = spans[256:384]
        ext[b1 + 512 : b1 + 640] = spans[128:256]
        ext[b1 + 640 : b1 + 768] = spans[0:128]
        ext[b1 + 128 : b1 + 256] = low[256:384]
        ext[b1 + 768 : b1 + 896] = up[256:384]
        b2 = BASE[2]
        ftmp[0:384] = low[0:384].astype(F32)
        ext[b1 : b1 + 128] = mean_rows(ftmp, 0, 128, 2).astype(BF16)
        ext[b2 + 384 : b2 + 448] = mean_rows(ftmp, 256, 64, 2).astype(BF16)
        ext[b2 + 448 : b2 + 512] = mean_rows(ftmp, 0, 64, 4).astype(BF16)
        ftmp[0:384] = up[0:384].astype(F32)
        ext[b1 + 896 : b1 + 1024] = mean_rows(ftmp, 0, 128, 2).astype(BF16)
        ext[b2 : b2 + 64] = mean_rows(ftmp, 0, 64, 4).astype(BF16)
        ext[b2 + 64 : b2 + 128] = mean_rows(ftmp, 256, 64, 2).astype(BF16)
        ext[b2 + 128 : b2 + 256] = low[384:512]
        ext[b2 + 256 : b2 + 384] = up[384:512]
        ext[BASE[3] : ROWS] = far[...]

    low_ok, up_ok = valid[0], valid[1]
    for level, row, rows, ok in (
        (0, 0, 256, low_ok), (0, 256, 1024, 1.0), (0, 1280, 256, up_ok),
        (1, 0, 256, low_ok), (1, 256, 512, 1.0), (1, 768, 256, up_ok),
        (2, 0, 128, up_ok), (2, 128, 128, low_ok), (2, 256, 128, up_ok), (2, 384, 128, low_ok),
        (3, 0, 128, valid[2]), (3, 128, 128, valid[3]), (3, 256, 128, valid[4]),
    ):
        at = slice(BASE[level] + row, BASE[level] + row + rows)
        scale = float(2**level)
        kt[:, at] = (kext[at] * scale).astype(BF16).T
        vals = (vext[at] * scale).astype(BF16).T
        top = lax.broadcasted_iota(jnp.int32, (16, rows), 0) == 0
        ones = jnp.where(top, ok * scale, 0.0).astype(BF16)
        for h in range(2):
            vt[h, 0:64, at] = vals[h * 64 : h * 64 + 64]
            vt[h, 64:80, at] = ones

    for b in range(4):
        at = slice(b * 256, b * 256 + 256)
        for h in range(2):
            to = slice((b * 2 + h) * 256, (b * 2 + h) * 256 + 256)
            mine = first if h == 0 else ~first
            qz[to] = jnp.where(mine, q[at].astype(F32) * 0.125, 0.0).astype(BF16)
            doz[to] = jnp.where(mine, do[at].astype(F32), 0.0).astype(BF16)

    for level, row, rows, col, b, nb in TILES:
        keys = kext[BASE[level] + row : BASE[level] + row + rows]
        for i in range(nb * 2):
            s = dot(keys, qz[(b * 2 + i) * 256 : (b * 2 + i) * 256 + 256], NT)
            es[level][row : row + rows, col + i * 256 : col + i * 256 + 256] = jnp.exp2(
                s * LOG2E
            ).astype(BF16)

    def finish_forward():
        least = jnp.full((1, 256), jnp.inf, F32)
        most = jnp.zeros((1, 256), F32)
        for b in range(4):
            at = slice(b * 256, b * 256 + 256)
            outs, recips = [], []
            for h in range(2):
                acc = jnp.zeros((80, 256), F32)
                for level, row, rows, col in pieces(b, h):
                    acc = acc + dot(
                        vt[h, :, BASE[level] + row : BASE[level] + row + rows],
                        es[level][row : row + rows, col : col + 256],
                    )
                total = acc[64:65]
                least = jnp.minimum(least, total)
                most = jnp.maximum(most, total)
                recip = 1.0 / total
                outs.append(acc[0:64] * recip)
                recips.append(recip)
                to = slice((b * 2 + h) * 256, (b * 2 + h) * 256 + 256)
                rls[0:1, to] = recip
            mixed = jnp.concatenate(outs, 0)
            o[at] = mixed.T.astype(BF16)
            prod = mixed.astype(BF16).astype(F32) * do[at].astype(F32).T
            wide = jnp.concatenate([jnp.broadcast_to(r, (64, 256)) for r in recips], 0).T
            for h in range(2):
                to = slice((b * 2 + h) * 256, (b * 2 + h) * 256 + 256)
                inn[0:1, to] = jnp.sum(prod[h * 64 : h * 64 + 64], axis=0, keepdims=True)
                mine = first if h == 0 else ~first
                dos[to] = jnp.where(mine, do[at].astype(F32) * wide, 0.0).astype(BF16)
                qs[to] = jnp.where(mine, q[at].astype(F32) * (wide * 0.125), 0.0).astype(BF16)
        fine = (jnp.min(least) > 2.0**-60) & (jnp.max(most) < 2.0**60)
        flag[0] = jnp.where(fine, 0, 1)

    finish_forward()

    @pl.when(flag[0] == 1)
    def _():
        oks = {
            0: (low_ok, 1.0, 1.0, 1.0, 1.0, up_ok),
            1: (low_ok, low_ok, 1.0, 1.0, 1.0, 1.0, up_ok, up_ok),
            2: (up_ok, low_ok, up_ok, low_ok),
            3: (valid[2], valid[3], valid[4]),
        }
        for b in range(4):
            for h in range(2):
                query = qz[(b * 2 + h) * 256 : (b * 2 + h) * 256 + 256]

                def scores(level, row, rows):
                    return dot(
                        kext[BASE[level] + row : BASE[level] + row + rows], query, NT
                    ) * LOG2E

                parts = []
                for level, row, rows, col in pieces(b, h):
                    step = 256 if level == 0 else 128
                    for r in range(row, row + rows, step):
                        parts.append((level, r, step, col, oks[level][r // step]))
                highest = jnp.full((1, 256), -jnp.inf, F32)
                for level, row, rows, col, ok in parts:
                    top = jnp.max(scores(level, row, rows), axis=0, keepdims=True)
                    highest = jnp.maximum(highest, jnp.where(ok > 0.5, top, -jnp.inf))
                for level, row, rows, col, ok in parts:
                    s = jnp.where(ok > 0.5, scores(level, row, rows) - highest, -200.0)
                    es[level][row : row + rows, col : col + 256] = jnp.exp2(s).astype(BF16)
        finish_forward()

    for level, row, rows, col, b, nb in TILES:
        vals = vext[BASE[level] + row : BASE[level] + row + rows]
        for i in range(nb * 2):
            to = slice((b * 2 + i) * 256, (b * 2 + i) * 256 + 256)
            at = (slice(row, row + rows), slice(col + i * 256, col + i * 256 + 256))
            dp = dot(vals, doz[to], NT) - inn[0:1, to]
            xs[level][at] = es[level][at] * dp.astype(BF16)

    for b in range(4):
        outs = []
        for h in range(2):
            acc = jnp.zeros((64, 256), F32)
            for level, row, rows, col in pieces(b, h):
                acc = acc + dot(
                    kt[h * 64 : h * 64 + 64, BASE[level] + row : BASE[level] + row + rows],
                    xs[level][row : row + rows, col : col + 256],
                )
            to = slice((b * 2 + h) * 256, (b * 2 + h) * 256 + 256)
            outs.append(acc * (rls[0:1, to] * 0.125))
        dq[b * 256 : b * 256 + 256] = jnp.concatenate(outs, 0).T.astype(BF16)

    for ws, right, own, low, up, far in (
        (xs, qs, gk, glk, guk, gfk), (es, dos, gv, glv, guv, gfv)
    ):
        got = {}
        for level, row, rows, col, b, nb in TILES:
            got[level, row] = dot(
                ws[level][row : row + rows, col : col + nb * 512],
                right[b * 512 : (b + nb) * 512],
            )
            if level == 0 and 0 < row < 1280:
                own[row - 256 : row] = got[level, row]
            elif level == 0:
                gtmp[0 if row == 0 else 384 : 256 if row == 0 else 640] = got[level, row]
            elif level == 1:
                g = got[level, row]
                if row == 0:
                    spread_rows(gtmp, 0, g, 2)
                elif row == 128:
                    gtmp[256:384] = g[0:128]
                    spread_rows(own, 768, g[128:256], 2)
                elif row == 384:
                    spread_rows(own, 512, g, 2)
                elif row == 512:
                    spread_rows(own, 256, g, 2)
                elif row == 640:
                    spread_rows(own, 0, g[0:128], 2)
                    gtmp[640:768] = g[128:256]
                else:
                    spread_rows(gtmp, 384, g, 2)
            elif level == 2:
                g = got[level, row]
                if row == 0:
                    spread_rows(gtmp, 384, g[0:64], 4)
                    spread_rows(gtmp, 640, g[64:128], 2)
                elif row == 128:
                    low[384:512] = g[0:128].astype(BF16)
                    up[384:512] = g[128:256].astype(BF16)
                else:
                    spread_rows(gtmp, 256, g[0:64], 2)
                    spread_rows(gtmp, 0, g[64:128], 4)
            else:
                far[...] = got[level, row].astype(BF16)
        low[0:384] = gtmp[0:384].astype(BF16)
        up[0:384] = gtmp[384:768].astype(BF16)


def moved(array, pairs):
    return lax.ppermute(array, AXES, pairs)


def shape(*dims, dtype=BF16):
    return jax.ShapeDtypeStruct(dims, dtype)


def vmem(limit):
    return pltpu.CompilerParams(vmem_limit_bytes=limit * 2**20)


def send(keys, values, start, pairs):
    col = start
    block = pl.BlockSpec((1024, PAIR), lambda j: (0, col + j))

    def body(k, v, up, down, far, tmp):
        for own, side in ((k, 0), (v, 1)):
            tmp[...] = own[...].astype(F32)
            up[side, 0:256] = own[768:1024]
            up[side, 256:384] = mean_rows(tmp, 512, 128, 2).astype(BF16)
            up[side, 384:512] = mean_rows(tmp, 0, 128, 4).astype(BF16)
            down[side, 0:256] = own[0:256]
            down[side, 256:384] = mean_rows(tmp, 256, 128, 2).astype(BF16)
            down[side, 384:512] = mean_rows(tmp, 512, 128, 4).astype(BF16)
            far[side] = mean_rows(tmp, 0, 128, 8).astype(BF16)

    side = lambda rows: pl.BlockSpec((2, rows, PAIR), lambda j: (0, 0, j))
    width = pairs * PAIR
    return pl.pallas_call(
        body,
        grid=(pairs,),
        in_specs=[block, block],
        out_specs=[side(512), side(512), side(128)],
        out_shape=[shape(2, 512, width), shape(2, 512, width), shape(2, 128, width)],
        scratch_shapes=[pltpu.VMEM((1024, PAIR), F32)],
        compiler_params=vmem(32),
        name="rows_to_send",
    )(keys, values)


def attend(valid, queries, keys, values, grad_out, low, up, far, start, pairs):
    whole = pl.BlockSpec((1024, PAIR), lambda j: (0, start + j))
    mine = pl.BlockSpec((1024, PAIR), lambda j: (0, j))

    def side(rows, which):
        return pl.BlockSpec((None, rows, PAIR), lambda j: (which, 0, j))

    width = pairs * PAIR

    def body(*refs):
        ins = refs[:11]
        o, dq, gk, gv, gl, gu, gf = refs[11:18]
        attend_kernel(
            *ins, o, dq, gk, gv,
            gl.at[0], gl.at[1], gu.at[0], gu.at[1], gf.at[0], gf.at[1], *refs[18:],
        )

    both = lambda rows: pl.BlockSpec((2, rows, PAIR), lambda j: (0, 0, j))
    return pl.pallas_call(
        body,
        grid=(pairs,),
        in_specs=[pl.BlockSpec(memory_space=pltpu.SMEM), whole, whole, whole, whole]
        + [side(rows, which) for rows in (512, 512, 384) for which in (0, 1)],
        out_specs=[mine, mine, mine, mine, both(512), both(512), both(384)],
        out_shape=[
            shape(1024, width), shape(1024, width),
            shape(1024, width, dtype=F32), shape(1024, width, dtype=F32),
            shape(2, 512, width), shape(2, 512, width), shape(2, 384, width),
        ],
        scratch_shapes=[
            pltpu.VMEM((ROWS, PAIR), BF16), pltpu.VMEM((ROWS, PAIR), BF16),
            pltpu.VMEM((PAIR, ROWS), BF16), pltpu.VMEM((2, 80, ROWS), BF16),
        ]
        + [
            pltpu.VMEM(dims, BF16)
            for dims in ((1536, 1536), (1024, 1024), (512, 2048), (384, 2048)) * 2
        ]
        + [pltpu.VMEM((2048, PAIR), BF16)] * 4
        + [
            pltpu.VMEM((8, 2048), F32), pltpu.VMEM((8, 2048), F32),
            pltpu.VMEM((1024, PAIR), F32), pltpu.VMEM((768, PAIR), F32),
            pltpu.SMEM((1,), jnp.int32),
        ],
        compiler_params=vmem(56),
        cost_estimate=pl.CostEstimate(
            flops=pairs * 14 * 10**9, bytes_accessed=pairs * 4 * 10**6, transcendentals=0
        ),
        name="attend_pairs",
    )(valid, queries, keys, values, grad_out, low, low, up, up, far, far)


def finish(own_k, own_v, above, below, far, pairs):
    mine = pl.BlockSpec((1024, PAIR), lambda j: (0, j))
    both = lambda rows: pl.BlockSpec((2, rows, PAIR), lambda j: (0, 0, j))

    def body(gk, gv, above, below, f0, f1, f2, dk, dv, tmp):
        for side, own, out in ((0, gk, dk), (1, gv, dv)):
            tmp[...] = own[...]
            tmp[768:1024] = tmp[768:1024] + above[side, 0:256].astype(F32)
            spread_rows(tmp, 512, above[side, 256:384].astype(F32), 2)
            spread_rows(tmp, 0, above[side, 384:512].astype(F32), 4)
            tmp[0:256] = tmp[0:256] + below[side, 0:256].astype(F32)
            spread_rows(tmp, 256, below[side, 256:384].astype(F32), 2)
            spread_rows(tmp, 512, below[side, 384:512].astype(F32), 4)
            total = f0[side].astype(F32) + f1[side].astype(F32) + f2[side].astype(F32)
            spread_rows(tmp, 0, total, 8)
            out[...] = tmp[...].astype(BF16)

    width = pairs * PAIR
    return pl.pallas_call(
        body,
        grid=(pairs,),
        in_specs=[mine, mine, both(512), both(512), both(128), both(128), both(128)],
        out_specs=[mine, mine],
        out_shape=[shape(1024, width), shape(1024, width)],
        scratch_shapes=[pltpu.VMEM((1024, PAIR), F32)],
        compiler_params=vmem(32),
        name="sum_grads",
    )(own_k, own_v, above, below, *far)


def local(queries, keys, values, grad_out):
    index = lax.axis_index(AXES)
    count = lax.axis_size(AXES)

    def by(step):
        return [(i, i + step) for i in range(count) if 0 <= i + step < count]

    three = [
        (i, i + (3 if i % 2 == 0 else -3))
        for i in range(count)
        if 0 <= i + (3 if i % 2 == 0 else -3) < count
    ]
    third = jnp.where(index % 2 == 0, index + 3, index - 3)
    valid = jnp.stack(
        [
            index > 0,
            index < count - 1,
            index >= 2,
            index < count - 2,
            (third >= 0) & (third < count),
        ]
    ).astype(F32)

    halos = []
    start = 0
    for pairs in GROUPS:
        up, down, far = send(keys, values, start, pairs)
        low = moved(up, by(1))
        high = moved(down, by(-1))
        spans = jnp.concatenate(
            [moved(far, by(2)), moved(far, by(-2)), moved(far, three)], axis=1
        )
        halos.append((start, pairs, low, high, spans))
        start += pairs

    results = []
    for start, pairs, low, high, spans in halos:
        o, dq, gk, gv, gl, gu, gf = attend(
            valid, queries, keys, values, grad_out, low, high, spans, start, pairs
        )
        above = moved(gl, by(-1))
        below = moved(gu, by(1))
        far = (
            moved(gf[:, 0:128], by(-2)),
            moved(gf[:, 128:256], by(2)),
            moved(gf[:, 256:384], [(b, a) for a, b in three]),
        )
        dk, dv = finish(gk, gv, above, below, far, pairs)
        results.append((o, dq, dk, dv))
    return tuple(jnp.concatenate(parts, axis=1) if len(parts) > 1 else parts[0]
                 for parts in zip(*results))


def solution(mesh):
    placed = P(AXES, None)
    return jax.shard_map(
        local,
        mesh=mesh,
        in_specs=(placed,) * 4,
        out_specs=(placed,) * 4,
        check_vma=False,
    )
```

```python
import math

import jax
import jax.numpy as jnp
from jax import lax
from jax.experimental import pallas as pl
from jax.experimental.pallas import tpu as pltpu
from jax.sharding import PartitionSpec as P

HEAD_DIM = 64
BLOCK = 256
HALF = 128
PAIR = 128
AXES = ("seqa", "seqb")
GROUPS = (2, 2, 2, 2)
ORDER = (
    ("pair", 0), ("cross", 0), ("pair", 1), ("cross", 1), ("pair", 2),
    ("attend", 0), ("cross", 2), ("pair", 3),
    ("attend", 1), ("cross", 3), ("back", 0),
    ("attend", 2), ("back", 1),
    ("attend", 3), ("back", 2), ("sum", 0), ("back", 3), ("sum", 1), ("sum", 2), ("sum", 3),
)
LIMIT = 60
LOG2E = math.log2(math.e)
BF16 = jnp.bfloat16
F32 = jnp.float32
NT = (((1,), (1,)), ((), ()))
NN = (((1,), (0,)), ((), ()))

BASE = (0, 1536, 2560, 3072)
ROWS = 3456

TILES = (
    (0, 0, 256, 1024, 0, 1),
    (0, 256, 256, 512, 0, 2),
    (0, 512, 256, 0, 0, 3),
    (0, 768, 256, 0, 1, 3),
    (0, 1024, 256, 0, 2, 2),
    (0, 1280, 256, 0, 3, 1),
    (1, 0, 128, 512, 1, 1),
    (1, 128, 256, 0, 0, 2),
    (1, 384, 128, 0, 0, 1),
    (1, 512, 128, 512, 3, 1),
    (1, 640, 256, 0, 2, 2),
    (1, 896, 128, 0, 2, 1),
    (2, 0, 128, 0, 0, 2),
    (2, 128, 256, 0, 0, 4),
    (2, 384, 128, 1024, 2, 2),
    (3, 0, 384, 0, 0, 4),
)


def pieces(b, h):
    at = h * 256
    low = (b // 2) * 512 + (1 - b % 2) * 128
    return (
        (0, b * 256, 256, 1024 + at),
        (0, b * 256 + 256, 256, 512 + at),
        (0, b * 256 + 512, 256, at),
        (1, low, 384, (b % 2) * 512 + at),
        (2, (b // 2) * 128, 384, b * 512 + at),
        (3, 0, 384, b * 512 + at),
    )


def dot(a, b, dims=NN):
    return lax.dot_general(a, b, dims, preferred_element_type=F32)


def mean_rows(rows, stride):
    step = min(256, rows.shape[0])
    out = lax.broadcasted_iota(jnp.int32, (step // stride, step), 0)
    at = lax.broadcasted_iota(jnp.int32, (step // stride, step), 1)
    take = jnp.where(at // stride == out, 1.0 / stride, 0.0).astype(BF16)
    parts = [dot(take, rows[i : i + step]) for i in range(0, rows.shape[0], step)]
    parts = [part.astype(BF16) for part in parts]
    return parts[0] if len(parts) == 1 else jnp.concatenate(parts, 0)


def repeat_rows(rows, stride):
    step = min(256 // stride, rows.shape[0])
    out = lax.broadcasted_iota(jnp.int32, (step * stride, step), 0)
    at = lax.broadcasted_iota(jnp.int32, (step * stride, step), 1)
    put = jnp.where(out // stride == at, 1.0, 0.0).astype(BF16)
    parts = [dot(put, rows[i : i + step]) for i in range(0, rows.shape[0], step)]
    return parts[0] if len(parts) == 1 else jnp.concatenate(parts, 0)


def add_rows(ref, start, rows, stride):
    at = slice(start, start + rows.shape[0] * stride)
    ref[at] = ref[at] + (repeat_rows(rows, stride) if stride > 1 else rows.astype(F32))


def spread_rows(ref, start, rows, stride):
    for i in range(stride):
        at = pl.ds(start + i, rows.shape[0], stride=stride)
        ref[at, :] = ref[at, :] + rows


def attend_kernel(
    role, valid, q, k, v, do, hk, hv, bk, bv, ak, av,
    o, dq, gk, gv, rh, rup, rdown, token,
    kext, vext, kt, vt, e0, e1, e2, e3, x0, x1, x2, x3,
    qz, doz, qs, dos, inn, rls, gtmp, cross, small, side, flag,
):
    es = (e0, e1, e2, e3)
    xs = (x0, x1, x2, x3)
    lane = lax.broadcasted_iota(jnp.int32, (256, PAIR), 1)
    first = lane < HEAD_DIM
    even = role[0] == 0
    odd = jnp.logical_not(even)
    pass_on(role, token)

    for which, (h, b, a) in enumerate(((hk, bk, ak), (hv, bv, av))):

        @pl.when(even)
        def _():
            cross[which] = b[...]
            small[which] = a[0:256]
            side[0, which] = b[0:512]
            side[1, which] = h[...]

        @pl.when(odd)
        def _():
            cross[which] = a[...]
            small[which] = b[0:256]
            side[0, which] = h[...]
            side[1, which] = a[0:512]

    for which, own, ext in ((0, k, kext), (1, v, vext)):
        low, up = side.at[0, which], side.at[1, which]
        ext[0:256] = low[0:256]
        ext[256:1280] = own[...]
        ext[1280:1536] = up[0:256]
        spans = mean_rows(own[...], 2)
        b1 = BASE[1]
        ext[b1 + 256 : b1 + 384] = spans[384:512]
        ext[b1 + 384 : b1 + 512] = spans[256:384]
        ext[b1 + 512 : b1 + 640] = spans[128:256]
        ext[b1 + 640 : b1 + 768] = spans[0:128]
        ext[b1 + 128 : b1 + 256] = low[256:384]
        ext[b1 + 768 : b1 + 896] = up[256:384]
        b2 = BASE[2]
        ext[b1 : b1 + 128] = mean_rows(low[0:256], 2)
        ext[b2 + 384 : b2 + 448] = mean_rows(low[256:384], 2)
        ext[b2 + 448 : b2 + 512] = mean_rows(low[0:256], 4)
        ext[b1 + 896 : b1 + 1024] = mean_rows(up[0:256], 2)
        ext[b2 : b2 + 64] = mean_rows(up[0:256], 4)
        ext[b2 + 64 : b2 + 128] = mean_rows(up[256:384], 2)
        ext[b2 + 128 : b2 + 256] = low[384:512]
        ext[b2 + 256 : b2 + 384] = up[384:512]
        ext[BASE[3] : BASE[3] + 128] = cross[which, 512:640]
        ext[BASE[3] + 128 : ROWS] = small[which]

    low_ok, up_ok = valid[0], valid[1]
    for level, row, rows, ok in (
        (0, 0, 256, low_ok), (0, 256, 1024, 1.0), (0, 1280, 256, up_ok),
        (1, 0, 256, low_ok), (1, 256, 512, 1.0), (1, 768, 256, up_ok),
        (2, 0, 128, up_ok), (2, 128, 128, low_ok), (2, 256, 128, up_ok), (2, 384, 128, low_ok),
        (3, 0, 128, valid[2]), (3, 128, 128, valid[3]), (3, 256, 128, valid[4]),
    ):
        at = slice(BASE[level] + row, BASE[level] + row + rows)
        scale = float(2**level)
        kt[:, at] = (kext[at] * scale).astype(BF16).T
        vals = (vext[at] * scale).astype(BF16).T
        top = lax.broadcasted_iota(jnp.int32, (16, rows), 0) == 0
        ones = jnp.where(top, ok * scale, 0.0).astype(BF16)
        for h in range(2):
            vt[h, 0:64, at] = vals[h * 64 : h * 64 + 64]
            vt[h, 64:80, at] = ones

    for b in range(4):
        at = slice(b * 256, b * 256 + 256)
        for h in range(2):
            to = slice((b * 2 + h) * 256, (b * 2 + h) * 256 + 256)
            mine = first if h == 0 else ~first
            qz[to] = jnp.where(mine, q[at].astype(F32) * 0.125, 0.0).astype(BF16)
            doz[to] = jnp.where(mine, do[at].astype(F32), 0.0).astype(BF16)

    for level, row, rows, col, b, nb in TILES:
        keys = kext[BASE[level] + row : BASE[level] + row + rows]
        for i in range(nb * 2):
            s = dot(keys, qz[(b * 2 + i) * 256 : (b * 2 + i) * 256 + 256], NT)
            es[level][row : row + rows, col + i * 256 : col + i * 256 + 256] = jnp.exp2(
                s * LOG2E
            ).astype(BF16)

    def finish_forward():
        least = jnp.full((1, 256), jnp.inf, F32)
        most = jnp.zeros((1, 256), F32)
        for b in range(4):
            at = slice(b * 256, b * 256 + 256)
            outs, recips = [], []
            for h in range(2):
                acc = jnp.zeros((80, 256), F32)
                for level, row, rows, col in pieces(b, h):
                    acc = acc + dot(
                        vt[h, :, BASE[level] + row : BASE[level] + row + rows],
                        es[level][row : row + rows, col : col + 256],
                    )
                total = acc[64:65]
                least = jnp.minimum(least, total)
                most = jnp.maximum(most, total)
                recip = 1.0 / total
                outs.append(acc[0:64] * recip)
                recips.append(recip)
                to = slice((b * 2 + h) * 256, (b * 2 + h) * 256 + 256)
                rls[0:1, to] = recip
            mixed = jnp.concatenate(outs, 0)
            o[at] = mixed.T.astype(BF16)
            prod = mixed.astype(BF16).astype(F32) * do[at].astype(F32).T
            wide = jnp.concatenate([jnp.broadcast_to(r, (64, 256)) for r in recips], 0).T
            for h in range(2):
                to = slice((b * 2 + h) * 256, (b * 2 + h) * 256 + 256)
                inn[0:1, to] = jnp.sum(prod[h * 64 : h * 64 + 64], axis=0, keepdims=True)
                mine = first if h == 0 else ~first
                dos[to] = jnp.where(mine, do[at].astype(F32) * wide, 0.0).astype(BF16)
                qs[to] = jnp.where(mine, q[at].astype(F32) * (wide * 0.125), 0.0).astype(BF16)
        fine = (jnp.min(least) > 2.0**-60) & (jnp.max(most) < 2.0**60)
        flag[0] = jnp.where(fine, 0, 1)

    finish_forward()

    @pl.when(flag[0] == 1)
    def _():
        oks = {
            0: (low_ok, 1.0, 1.0, 1.0, 1.0, up_ok),
            1: (low_ok, low_ok, 1.0, 1.0, 1.0, 1.0, up_ok, up_ok),
            2: (up_ok, low_ok, up_ok, low_ok),
            3: (valid[2], valid[3], valid[4]),
        }
        for b in range(4):
            for h in range(2):
                query = qz[(b * 2 + h) * 256 : (b * 2 + h) * 256 + 256]

                def scores(level, row, rows):
                    return dot(
                        kext[BASE[level] + row : BASE[level] + row + rows], query, NT
                    ) * LOG2E

                parts = []
                for level, row, rows, col in pieces(b, h):
                    step = 256 if level == 0 else 128
                    for r in range(row, row + rows, step):
                        parts.append((level, r, step, col, oks[level][r // step]))
                highest = jnp.full((1, 256), -jnp.inf, F32)
                for level, row, rows, col, ok in parts:
                    top = jnp.max(scores(level, row, rows), axis=0, keepdims=True)
                    highest = jnp.maximum(highest, jnp.where(ok > 0.5, top, -jnp.inf))
                for level, row, rows, col, ok in parts:
                    s = jnp.where(ok > 0.5, scores(level, row, rows) - highest, -200.0)
                    es[level][row : row + rows, col : col + 256] = jnp.exp2(s).astype(BF16)
        finish_forward()

    for level, row, rows, col, b, nb in TILES:
        vals = vext[BASE[level] + row : BASE[level] + row + rows]
        for i in range(nb * 2):
            to = slice((b * 2 + i) * 256, (b * 2 + i) * 256 + 256)
            at = (slice(row, row + rows), slice(col + i * 256, col + i * 256 + 256))
            dp = dot(vals, doz[to], NT) - inn[0:1, to]
            xs[level][at] = es[level][at] * dp.astype(BF16)

    for b in range(4):
        outs = []
        for h in range(2):
            acc = jnp.zeros((64, 256), F32)
            for level, row, rows, col in pieces(b, h):
                acc = acc + dot(
                    kt[h * 64 : h * 64 + 64, BASE[level] + row : BASE[level] + row + rows],
                    xs[level][row : row + rows, col : col + 256],
                )
            to = slice((b * 2 + h) * 256, (b * 2 + h) * 256 + 256)
            outs.append(acc * (rls[0:1, to] * 0.125))
        dq[b * 256 : b * 256 + 256] = jnp.concatenate(outs, 0).T.astype(BF16)

    for which, ws, right, own in ((0, xs, qs, gk), (1, es, dos, gv)):
        low, up = side.at[0, which], side.at[1, which]
        got = {}
        for level, row, rows, col, b, nb in TILES:
            got[level, row] = dot(
                ws[level][row : row + rows, col : col + nb * 512],
                right[b * 512 : (b + nb) * 512],
            )
            if level == 0 and 0 < row < 1280:
                own[row - 256 : row] = got[level, row]
            elif level == 0:
                gtmp[0 if row == 0 else 384 : 256 if row == 0 else 640] = got[level, row]
            elif level == 1:
                g = got[level, row]
                if row == 0:
                    spread_rows(gtmp, 0, g, 2)
                elif row == 128:
                    gtmp[256:384] = g[0:128]
                    spread_rows(own, 768, g[128:256], 2)
                elif row == 384:
                    spread_rows(own, 512, g, 2)
                elif row == 512:
                    spread_rows(own, 256, g, 2)
                elif row == 640:
                    spread_rows(own, 0, g[0:128], 2)
                    gtmp[640:768] = g[128:256]
                else:
                    spread_rows(gtmp, 384, g, 2)
            elif level == 2:
                g = got[level, row]
                if row == 0:
                    spread_rows(gtmp, 384, g[0:64], 4)
                    spread_rows(gtmp, 640, g[64:128], 2)
                elif row == 128:
                    low[384:512] = g[0:128].astype(BF16)
                    up[384:512] = g[128:256].astype(BF16)
                else:
                    spread_rows(gtmp, 256, g[0:64], 2)
                    spread_rows(gtmp, 0, g[64:128], 4)
            else:
                cross[which, 512:640] = got[level, row][0:128].astype(BF16)
                small[which] = got[level, row][128:384].astype(BF16)
        low[0:384] = gtmp[0:384].astype(BF16)
        up[0:384] = gtmp[384:768].astype(BF16)

        @pl.when(even)
        def _():
            rh[which] = up[...]
            rdown[which, 0:512] = low[...]
            rdown[which, 512:640] = cross[which, 512:640]
            rup[which, 0:256] = small[which]

        @pl.when(odd)
        def _():
            rh[which] = low[...]
            rup[which, 0:512] = up[...]
            rup[which, 512:640] = cross[which, 512:640]
            rdown[which, 0:256] = small[which]


def pass_on(role, token):
    token[0] = role[0]
    token[1] = role[1]


def add_down(ref, rows, own):
    add_rows(ref, 0, rows[0:256], 1)
    if own:
        add_rows(ref, 256, rows[256:384], 2)
        add_rows(ref, 512, rows[384:512], 4)
    else:
        add_rows(ref, 512, rows[256:384], 1)
        add_rows(ref, 640, rows[384:448], 2)
        add_rows(ref, 256, rows[448:512], 4)


def add_up(ref, rows, own):
    if own:
        add_rows(ref, 768, rows[0:256], 1)
        add_rows(ref, 512, rows[256:384], 2)
        add_rows(ref, 0, rows[384:512], 4)
    else:
        add_rows(ref, 256, rows[0:256], 1)
        add_rows(ref, 640, rows[256:384], 1)
        add_rows(ref, 0, rows[384:448], 4)
        add_rows(ref, 512, rows[448:512], 2)


def moved(array, pairs):
    return lax.ppermute(array, AXES, pairs)


def shape(*dims, dtype=BF16):
    return jax.ShapeDtypeStruct(dims, dtype)


def vmem(limit):
    return pltpu.CompilerParams(vmem_limit_bytes=limit * 2**20)


SMEM = pl.BlockSpec(memory_space=pltpu.SMEM)


def both(rows):
    return pl.BlockSpec((2, rows, PAIR), lambda j: (0, 0, j))


def columns(start):
    return pl.BlockSpec((1024, PAIR), lambda j: (0, start + j))


TOKEN = shape(2, dtype=jnp.int32)


def pair_rows(role, keys, values, start, pairs):
    def body(role, k, v, out, token):
        pass_on(role, token)
        for which, own in ((0, k), (1, v)):
            out[which, 0:256] = own[0:256]
            out[which, 256:512] = own[768:1024]
            out[which, 512:768] = mean_rows(own[256:768], 2)

    return pl.pallas_call(
        body,
        grid=(pairs,),
        in_specs=[SMEM] + [columns(start)] * 2,
        out_specs=[both(768), SMEM],
        out_shape=[shape(2, 768, pairs * PAIR), TOKEN],
        compiler_params=vmem(LIMIT),
        name="pair_rows",
    )(role, keys, values)


def cross_rows(role, keys, values, partner, start, pairs):
    def body(role, k, v, p, near, up_out, down_out, token, spans):
        even, wrap = role[0] == 0, role[1]
        odd = jnp.logical_not(even)
        pass_on(role, token)

        for which, own in ((0, k), (1, v)):
            spans[0:128] = mean_rows(own[...], 8)
            spans[128:160] = mean_rows(p[which, 0:256], 8)
            spans[160:192] = mean_rows(p[which, 512:640], 4)
            spans[192:224] = mean_rows(p[which, 640:768], 4)
            spans[224:256] = mean_rows(p[which, 256:512], 8)

            def theirs_down(out):
                out[which, 0:256] = p[which, 0:256]
                out[which, 256:384] = p[which, 512:640]
                out[which, 384:448] = mean_rows(p[which, 640:768], 2)
                out[which, 448:512] = mean_rows(p[which, 256:512], 4)

            def theirs_up(out):
                out[which, 0:256] = p[which, 256:512]
                out[which, 256:384] = p[which, 640:768]
                out[which, 384:448] = mean_rows(p[which, 0:256], 4)
                out[which, 448:512] = mean_rows(p[which, 512:640], 2)

            @pl.when(even)
            def _():
                theirs_down(near)
                theirs_up(up_out)
                up_out[which, 512:640] = spans[0:128]
                down_out[which, 0:256] = spans[...]

            @pl.when(odd)
            def _():
                theirs_up(near)
                theirs_down(down_out)
                down_out[which, 512:640] = spans[0:128]
                up_out[which, 0:256] = spans[...]

            @pl.when((wrap == 1) & even)
            def _():
                down_out[which, 0:256] = own[0:256]
                down_out[which, 256:384] = mean_rows(own[256:512], 2)
                down_out[which, 384:512] = mean_rows(own[512:1024], 4)
                down_out[which, 512:640] = spans[128:256]

            @pl.when((wrap == 1) & odd)
            def _():
                up_out[which, 0:256] = own[768:1024]
                up_out[which, 256:384] = mean_rows(own[512:768], 2)
                up_out[which, 384:512] = mean_rows(own[0:512], 4)
                up_out[which, 512:640] = spans[128:256]

            @pl.when((wrap == 2) & even)
            def _():
                up_out[which, 0:128] = spans[128:256]
                up_out[which, 128:256] = spans[0:128]

            @pl.when((wrap == 2) & odd)
            def _():
                down_out[which, 0:128] = spans[128:256]
                down_out[which, 128:256] = spans[0:128]

    width = pairs * PAIR
    return pl.pallas_call(
        body,
        grid=(pairs,),
        in_specs=[SMEM, columns(start), columns(start), both(768)],
        out_specs=[both(512), both(640), both(640), SMEM],
        out_shape=[shape(2, rows, width) for rows in (512, 640, 640)] + [TOKEN],
        scratch_shapes=[pltpu.VMEM((256, PAIR), BF16)],
        compiler_params=vmem(LIMIT),
        name="cross_rows",
    )(role, keys, values, partner)


def attend(role, valid, queries, keys, values, grad_out, came, before, start, pairs):
    width = pairs * PAIR

    def side(rows, which):
        return pl.BlockSpec((None, rows, PAIR), lambda j: (which, 0, j))

    extra = 0 if before is None else 2

    def body(*refs):
        attend_kernel(*refs[:12], *refs[12 + extra :])

    heights = (512, 640, 640)
    whole = shape(1024, queries.shape[1])
    return pl.pallas_call(
        body,
        grid=(pairs,),
        in_specs=[SMEM, SMEM] + [columns(start)] * 4
        + [side(rows, which) for rows in heights for which in (0, 1)]
        + [pl.BlockSpec(memory_space=pl.ANY)] * extra,
        out_specs=[columns(start)] * 2 + [columns(0)] * 2 + [both(rows) for rows in heights]
        + [SMEM],
        out_shape=[whole, whole]
        + [shape(1024, width, dtype=F32)] * 2
        + [shape(2, rows, width) for rows in heights]
        + [TOKEN],
        input_output_aliases={12: 0, 13: 1} if extra else {},
        scratch_shapes=[
            pltpu.VMEM((ROWS, PAIR), BF16), pltpu.VMEM((ROWS, PAIR), BF16),
            pltpu.VMEM((PAIR, ROWS), BF16), pltpu.VMEM((2, 80, ROWS), BF16),
        ]
        + [
            pltpu.VMEM(dims, BF16)
            for dims in ((1536, 1536), (1024, 1024), (512, 2048), (384, 2048)) * 2
        ]
        + [pltpu.VMEM((2048, PAIR), BF16)] * 4
        + [
            pltpu.VMEM((8, 2048), F32), pltpu.VMEM((8, 2048), F32),
            pltpu.VMEM((768, PAIR), F32),
            pltpu.VMEM((2, 640, PAIR), BF16), pltpu.VMEM((2, 256, PAIR), BF16),
            pltpu.VMEM((2, 2, 512, PAIR), BF16),
            pltpu.SMEM((1,), jnp.int32),
        ],
        compiler_params=vmem(LIMIT),
        cost_estimate=pl.CostEstimate(
            flops=pairs * 14 * 10**9, bytes_accessed=pairs * 4 * 10**6, transcendentals=0
        ),
        name="attend_pairs",
    )(
        role, valid, queries, keys, values, grad_out,
        *[part for pair in came for part in (pair, pair)], *(before or ()),
    )


def pair_grads(role, near, above, below, pairs):
    def body(role, near, above, below, out, token, tmp):
        even, wrap = role[0] == 0, role[1]
        odd = jnp.logical_not(even)
        pass_on(role, token)

        def add_span(rows):
            add_rows(tmp, 0, rows[0:32], 8)
            add_rows(tmp, 512, rows[32:64], 4)
            add_rows(tmp, 640, rows[64:96], 4)
            add_rows(tmp, 256, rows[96:128], 8)

        for which in (0, 1):
            tmp[...] = jnp.zeros_like(tmp)

            @pl.when(even)
            def _():
                add_down(tmp, near[which], False)

                @pl.when(wrap != 2)
                def _():
                    add_up(tmp, above[which, 0:512], False)

                @pl.when(wrap == 2)
                def _():
                    add_span(above[which, 0:128])

                @pl.when(wrap == 1)
                def _():
                    add_span(below[which, 512:640])

                @pl.when(wrap != 1)
                def _():
                    add_span(below[which, 128:256])

            @pl.when(odd)
            def _():
                add_up(tmp, near[which], False)

                @pl.when(wrap != 2)
                def _():
                    add_down(tmp, below[which, 0:512], False)

                @pl.when(wrap == 2)
                def _():
                    add_span(below[which, 0:128])

                @pl.when(wrap == 1)
                def _():
                    add_span(above[which, 512:640])

                @pl.when(wrap != 1)
                def _():
                    add_span(above[which, 128:256])

            out[which] = tmp[...].astype(BF16)

    return pl.pallas_call(
        body,
        grid=(pairs,),
        in_specs=[SMEM, both(512), both(640), both(640)],
        out_specs=[both(768), SMEM],
        out_shape=[shape(2, 768, pairs * PAIR), TOKEN],
        scratch_shapes=[pltpu.VMEM((768, PAIR), F32)],
        compiler_params=vmem(LIMIT),
        name="pair_grads",
    )(role, near, above, below)


def finish(role, own_k, own_v, above, below, partner, before, start, pairs):
    extra = 0 if before is None else 2

    def body(*refs):
        role, gk, gv, above, below, got = refs[:6]
        dk, dv, token, tmp = refs[6 + extra :]
        even, wrap = role[0] == 0, role[1]
        odd = jnp.logical_not(even)
        pass_on(role, token)
        for which, own, out in ((0, gk, dk), (1, gv, dv)):
            tmp[...] = own[...]
            add_rows(tmp, 0, got[which, 0:256], 1)
            add_rows(tmp, 768, got[which, 256:512], 1)
            add_rows(tmp, 256, got[which, 512:768], 2)

            for here, large, small, add in ((even, above, below, add_down), (odd, below, above, add_up)):

                @pl.when(here & (wrap != 2))
                def _():
                    add_rows(tmp, 0, large[which, 512:640], 8)

                @pl.when(here & (wrap == 2))
                def _():
                    add_rows(tmp, 0, large[which, 128:256], 8)

                @pl.when(here & (wrap != 1))
                def _():
                    add_rows(tmp, 0, small[which, 0:128], 8)

                @pl.when(here & (wrap == 1))
                def _():
                    add(tmp, small[which, 0:512], True)

            out[...] = tmp[...].astype(BF16)

    whole = shape(1024, 1024)
    return pl.pallas_call(
        body,
        grid=(pairs,),
        in_specs=[SMEM] + [columns(0)] * 2 + [both(640), both(640), both(768)]
        + [pl.BlockSpec(memory_space=pl.ANY)] * extra,
        out_specs=[columns(start)] * 2 + [SMEM],
        out_shape=[whole, whole, TOKEN],
        input_output_aliases={6: 0, 7: 1} if extra else {},
        scratch_shapes=[pltpu.VMEM((1024, PAIR), F32)],
        compiler_params=vmem(LIMIT),
        name="sum_grads",
    )(role, own_k, own_v, above, below, partner, *(before or ()))


def routes(outer, inner):
    count = outer * inner
    up = {i: i + 2 for i in range(count - 2)}
    for a in range(1, outer - 1, 2):
        last = a * inner + inner - 2
        up[last], up[last + 1] = last + 3, last + 2
    return [(i, i ^ 1) for i in range(count)], sorted(up.items())


def local(queries, keys, values, grad_out):
    a, b = lax.axis_index(AXES[0]), lax.axis_index(AXES[1])
    outer, inner = lax.axis_size(AXES[0]), lax.axis_size(AXES[1])
    index = a * inner + b
    count = outer * inner
    partners, up = routes(outer, inner)
    down = [(j, i) for i, j in up]
    above = (a % 2 == 1) & (a < outer - 1) & (b >= inner - 2)
    below = (a % 2 == 0) & (a > 0) & (b < 2)
    ends = (b == 0) | (b == inner - 1)
    odd = index % 2
    wrap = jnp.where(above | below, jnp.where(ends, 1, 2), 0)
    token = jnp.stack([odd, wrap]).astype(jnp.int32)
    sign = 1 - 2 * odd

    def there(step):
        at = index + step * sign
        return (at >= 0) & (at < count)

    valid = jnp.stack(
        [index > 0, index < count - 1, there(-2), there(2), there(3)]
    ).astype(F32)

    starts = [sum(GROUPS[:i]) for i in range(len(GROUPS))]
    partner, came, grown, near, answers, returned = {}, {}, {}, {}, {}, {}
    mixed = grads = None
    for step, i in ORDER:
        start, pairs = starts[i], GROUPS[i]
        if step == "pair":
            rows, token = pair_rows(token, keys, values, start, pairs)
            partner[i] = moved(rows, partners)
        elif step == "cross":
            side, upward, downward, token = cross_rows(
                token, keys, values, partner[i], start, pairs
            )
            came[i] = (side, moved(upward, up), moved(downward, down))
        elif step == "attend":
            *mixed, gk, gv, near[i], upward, downward, token = attend(
                token, valid, queries, keys, values, grad_out, came[i], mixed, start, pairs
            )
            grown[i] = (gk, gv)
            answers[i] = (moved(downward, down), moved(upward, up))
        elif step == "back":
            rows, token = pair_grads(token, near[i], *answers[i], pairs)
            returned[i] = moved(rows, partners)
        else:
            *grads, token = finish(token, *grown[i], *answers[i], returned[i], grads, start, pairs)
    return (*mixed, *grads)


def solution(mesh):
    placed = P(AXES, None)
    return jax.shard_map(
        local,
        mesh=mesh,
        in_specs=(placed,) * 4,
        out_specs=(placed,) * 4,
        check_vma=False,
    )
```

```python
import math

import jax
import jax.numpy as jnp
from jax import lax
from jax.experimental import pallas as pl
from jax.experimental.pallas import tpu as pltpu
from jax.sharding import PartitionSpec as P

HEAD_DIM = 64
BLOCK = 256
HALF = 128
PAIR = 128
AXES = ("seqa", "seqb")
GROUPS = (1, 2, 3, 2)
ORDER = (
    ("pair", 0), ("cross", 0), ("pair", 1), ("cross", 1), ("pair", 2),
    ("attend", 0), ("cross", 2), ("pair", 3),
    ("attend", 1), ("cross", 3), ("back", 0),
    ("attend", 2), ("back", 1),
    ("attend", 3), ("back", 2), ("sum", 0), ("back", 3), ("sum", 1), ("sum", 2), ("sum", 3),
)
LIMIT = 60
LOG2E = math.log2(math.e)
BF16 = jnp.bfloat16
F32 = jnp.float32
NT = (((1,), (1,)), ((), ()))
NN = (((1,), (0,)), ((), ()))

BASE = (0, 1536, 2560, 3072)
ROWS = 3456

PIECES = ((768, 0), (384, 768), (384, 1152), (384, 1536))


def piece_starts(b):
    half = b // 2
    first = BASE[1] + half * 512 + (1 - (b - 2 * half)) * 128
    rows = (b * 256, first, BASE[2] + half * 128, BASE[3])
    return [r if isinstance(r, int) else pl.multiple_of(r, 128) for r in rows]


def dot(a, b, dims=NN):
    return lax.dot_general(a, b, dims, preferred_element_type=F32)


def mean_rows(ref, start, count, stride):
    total = ref[pl.ds(start, count, stride=stride), :]
    for i in range(1, stride):
        total = total + ref[pl.ds(start + i, count, stride=stride), :]
    return (total * (1.0 / stride)).astype(BF16)


def add_rows(ref, start, rows, stride):
    if stride == 1:
        at = slice(start, start + rows.shape[0])
        ref[at] = ref[at] + rows.astype(F32)
    else:
        spread_rows(ref, start, rows.astype(F32), stride)


def spread_rows(ref, start, rows, stride):
    for i in range(stride):
        at = pl.ds(start + i, rows.shape[0], stride=stride)
        ref[at, :] = ref[at, :] + rows


def attend_kernel(
    role, valid, q, k, v, do, hk, hv, bk, bv, ak, av,
    o, dq, gk, gv, rh, rup, rdown, token,
    kext, vext, kt, vt, e, x, qz, doz, qs, dos, acck, accv, inn, rls, ftmp, gtmp,
    cross, small, side, flag, oks,
):
    lane = lax.broadcasted_iota(jnp.int32, (256, PAIR), 1)
    first = lane < HEAD_DIM
    even = role[0] == 0
    odd = jnp.logical_not(even)
    pass_on(role, token)

    for which, (h, b, a) in enumerate(((hk, bk, ak), (hv, bv, av))):

        @pl.when(even)
        def _():
            cross[which] = b[...]
            small[which] = a[0:256]
            side[0, which] = b[0:512]
            side[1, which] = h[...]

        @pl.when(odd)
        def _():
            cross[which] = a[...]
            small[which] = b[0:256]
            side[0, which] = h[...]
            side[1, which] = a[0:512]

    for which, own, ext in ((0, k, kext), (1, v, vext)):
        low, up = side.at[0, which], side.at[1, which]
        ext[0:256] = low[0:256]
        ext[256:1280] = own[...]
        ext[1280:1536] = up[0:256]
        ftmp[...] = own[...].astype(F32)
        spans = mean_rows(ftmp, 0, 512, 2)
        b1 = BASE[1]
        ext[b1 + 256 : b1 + 384] = spans[384:512]
        ext[b1 + 384 : b1 + 512] = spans[256:384]
        ext[b1 + 512 : b1 + 640] = spans[128:256]
        ext[b1 + 640 : b1 + 768] = spans[0:128]
        ext[b1 + 128 : b1 + 256] = low[256:384]
        ext[b1 + 768 : b1 + 896] = up[256:384]
        b2 = BASE[2]
        ftmp[0:384] = low[0:384].astype(F32)
        ext[b1 : b1 + 128] = mean_rows(ftmp, 0, 128, 2)
        ext[b2 + 384 : b2 + 448] = mean_rows(ftmp, 256, 64, 2)
        ext[b2 + 448 : b2 + 512] = mean_rows(ftmp, 0, 64, 4)
        ftmp[0:384] = up[0:384].astype(F32)
        ext[b1 + 896 : b1 + 1024] = mean_rows(ftmp, 0, 128, 2)
        ext[b2 : b2 + 64] = mean_rows(ftmp, 0, 64, 4)
        ext[b2 + 64 : b2 + 128] = mean_rows(ftmp, 256, 64, 2)
        ext[b2 + 128 : b2 + 256] = low[384:512]
        ext[b2 + 256 : b2 + 384] = up[384:512]
        ext[BASE[3] : BASE[3] + 128] = cross[which, 512:640]
        ext[BASE[3] + 128 : ROWS] = small[which]

    low_ok, up_ok = valid[0], valid[1]
    for level, row, rows, ok in (
        (0, 0, 256, low_ok), (0, 256, 1024, 1.0), (0, 1280, 256, up_ok),
        (1, 0, 256, low_ok), (1, 256, 512, 1.0), (1, 768, 256, up_ok),
        (2, 0, 128, up_ok), (2, 128, 128, low_ok), (2, 256, 128, up_ok), (2, 384, 128, low_ok),
        (3, 0, 128, valid[2]), (3, 128, 128, valid[3]), (3, 256, 128, valid[4]),
    ):
        at = slice(BASE[level] + row, BASE[level] + row + rows)
        for i in range(at.start // 128, at.stop // 128):
            oks[i] = ok
        scale = float(2**level)
        kt[:, at] = (kext[at] * scale).astype(BF16).T
        vals = (vext[at] * scale).astype(BF16).T
        top = lax.broadcasted_iota(jnp.int32, (16, rows), 0) == 0
        ones = jnp.where(top, ok * scale, 0.0).astype(BF16)
        for h in range(2):
            vt[h, 0:64, at] = vals[h * 64 : h * 64 + 64]
            vt[h, 64:80, at] = ones

    acck[...] = jnp.zeros_like(acck)
    accv[...] = jnp.zeros_like(accv)

    def block_step(b, carry):
        at = pl.ds(pl.multiple_of(b * 256, 256), 256)
        starts = piece_starts(b)
        spots = [(pl.ds(r, n), slice(to, to + n)) for r, (n, to) in zip(starts, PIECES)]
        query, grad = q[at].astype(F32), do[at].astype(F32)
        heads = (slice(0, 256), slice(256, 512))
        for h in range(2):
            mine = first if h == 0 else ~first
            qz[heads[h]] = jnp.where(mine, query * 0.125, 0.0).astype(BF16)
            doz[heads[h]] = jnp.where(mine, grad, 0.0).astype(BF16)

        for rows, to in spots:
            for h in heads:
                s = dot(kext[rows], qz[h], NT)
                e[to, h] = jnp.exp2(s * LOG2E).astype(BF16)

        def forward():
            outs, recips = [], []
            least, most = None, None
            for h in range(2):
                acc = jnp.zeros((80, 256), F32)
                for rows, to in spots:
                    acc = acc + dot(vt[h, :, rows], e[to, heads[h]])
                total = acc[64:65]
                least = total if least is None else jnp.minimum(least, total)
                most = total if most is None else jnp.maximum(most, total)
                recip = 1.0 / total
                outs.append(acc[0:64] * recip)
                recips.append(recip)
            fine = (jnp.min(least) > 2.0**-60) & (jnp.max(most) < 2.0**60)
            flag[0] = jnp.where(fine, 0, 1)
            return outs, recips

        def settle(outs, recips):
            mixed = jnp.concatenate(outs, 0)
            o[at] = mixed.T.astype(BF16)
            prod = mixed.astype(BF16).astype(F32) * grad.T
            wide = jnp.concatenate([jnp.broadcast_to(r, (64, 256)) for r in recips], 0).T
            for h in range(2):
                inn[0:1, heads[h]] = jnp.sum(prod[h * 64 : h * 64 + 64], axis=0, keepdims=True)
                rls[0:1, heads[h]] = recips[h]
                mine = first if h == 0 else ~first
                dos[heads[h]] = jnp.where(mine, grad * wide, 0.0).astype(BF16)
                qs[heads[h]] = jnp.where(mine, query * (wide * 0.125), 0.0).astype(BF16)

        settle(*forward())

        @pl.when(flag[0] == 1)
        def _():
            for h in heads:

                def scores(row):
                    row = pl.multiple_of(row, 128)
                    s = dot(kext[pl.ds(row, 128)], qz[h], NT) * LOG2E
                    return jnp.where(oks[row // 128] > 0.5, s, -jnp.inf)

                highest = jnp.full((1, 256), -jnp.inf, F32)
                for r, (n, to) in zip(starts, PIECES):
                    highest = lax.fori_loop(
                        0,
                        n // 128,
                        lambda t, top: jnp.maximum(
                            top, jnp.max(scores(r + t * 128), axis=0, keepdims=True)
                        ),
                        highest,
                    )
                for r, (n, to) in zip(starts, PIECES):

                    def again(t, carry):
                        put = pl.ds(pl.multiple_of(to + t * 128, 128), 128)
                        e[put, h] = jnp.exp2(scores(r + t * 128) - highest).astype(BF16)
                        return carry

                    lax.fori_loop(0, n // 128, again, 0)
            settle(*forward())

        for rows, to in spots:
            for h in heads:
                dp = dot(vext[rows], doz[h], NT) - inn[0:1, h]
                x[to, h] = e[to, h] * dp.astype(BF16)

        outs = []
        for h in range(2):
            acc = jnp.zeros((64, 256), F32)
            for rows, to in spots:
                acc = acc + dot(kt[h * 64 : h * 64 + 64, rows], x[to, heads[h]])
            outs.append(acc * (rls[0:1, heads[h]] * 0.125))
        dq[at] = jnp.concatenate(outs, 0).T.astype(BF16)

        for rows, to in spots:
            acck[rows] = acck[rows] + dot(x[to], qs[...])
            accv[rows] = accv[rows] + dot(e[to], dos[...])
        return carry

    lax.fori_loop(0, 4, block_step, 0)

    b1, b2, b3 = BASE[1:]
    for which, acc, own in ((0, acck, gk), (1, accv, gv)):
        low, up = side.at[0, which], side.at[1, which]
        own[...] = acc[256:1280]
        for i, row in enumerate((640, 512, 384, 256)):
            spread_rows(own, i * 256, acc[b1 + row : b1 + row + 128], 2)
        gtmp[0:256] = acc[0:256]
        spread_rows(gtmp, 0, acc[b1 : b1 + 128], 2)
        spread_rows(gtmp, 0, acc[b2 + 448 : b2 + 512], 4)
        gtmp[256:384] = acc[b1 + 128 : b1 + 256]
        spread_rows(gtmp, 256, acc[b2 + 384 : b2 + 448], 2)
        gtmp[384:640] = acc[1280:1536]
        spread_rows(gtmp, 384, acc[b1 + 896 : b1 + 1024], 2)
        spread_rows(gtmp, 384, acc[b2 : b2 + 64], 4)
        gtmp[640:768] = acc[b1 + 768 : b1 + 896]
        spread_rows(gtmp, 640, acc[b2 + 64 : b2 + 128], 2)
        low[0:384] = gtmp[0:384].astype(BF16)
        up[0:384] = gtmp[384:768].astype(BF16)
        low[384:512] = acc[b2 + 128 : b2 + 256].astype(BF16)
        up[384:512] = acc[b2 + 256 : b2 + 384].astype(BF16)
        cross[which, 512:640] = acc[b3 : b3 + 128].astype(BF16)
        small[which] = acc[b3 + 128 : ROWS].astype(BF16)

        @pl.when(even)
        def _():
            rh[which] = up[...]
            rdown[which, 0:512] = low[...]
            rdown[which, 512:640] = cross[which, 512:640]
            rup[which, 0:256] = small[which]

        @pl.when(odd)
        def _():
            rh[which] = low[...]
            rup[which, 0:512] = up[...]
            rup[which, 512:640] = cross[which, 512:640]
            rdown[which, 0:256] = small[which]


def pass_on(role, token):
    token[0] = role[0]
    token[1] = role[1]


def add_down(ref, rows, own):
    add_rows(ref, 0, rows[0:256], 1)
    if own:
        add_rows(ref, 256, rows[256:384], 2)
        add_rows(ref, 512, rows[384:512], 4)
    else:
        add_rows(ref, 512, rows[256:384], 1)
        add_rows(ref, 640, rows[384:448], 2)
        add_rows(ref, 256, rows[448:512], 4)


def add_up(ref, rows, own):
    if own:
        add_rows(ref, 768, rows[0:256], 1)
        add_rows(ref, 512, rows[256:384], 2)
        add_rows(ref, 0, rows[384:512], 4)
    else:
        add_rows(ref, 256, rows[0:256], 1)
        add_rows(ref, 640, rows[256:384], 1)
        add_rows(ref, 0, rows[384:448], 4)
        add_rows(ref, 512, rows[448:512], 2)


def moved(array, pairs):
    return lax.ppermute(array, AXES, pairs)


def shape(*dims, dtype=BF16):
    return jax.ShapeDtypeStruct(dims, dtype)


def vmem(limit):
    return pltpu.CompilerParams(vmem_limit_bytes=limit * 2**20)


SMEM = pl.BlockSpec(memory_space=pltpu.SMEM)


def both(rows):
    return pl.BlockSpec((None, 2, rows, PAIR), lambda j: (j, 0, 0, 0))


def own_rows():
    return pl.BlockSpec((None, 1024, PAIR), lambda j: (j, 0, 0))


def columns(start):
    return pl.BlockSpec((1024, PAIR), lambda j: (0, start + j))


TOKEN = shape(2, dtype=jnp.int32)


def pair_rows(role, keys, values, start, pairs):
    def body(role, k, v, out, token, tmp):
        pass_on(role, token)
        for which, own in ((0, k), (1, v)):
            tmp[...] = own[256:768].astype(F32)
            out[which, 0:256] = own[0:256]
            out[which, 256:512] = own[768:1024]
            out[which, 512:768] = mean_rows(tmp, 0, 256, 2)

    return pl.pallas_call(
        body,
        grid=(pairs,),
        in_specs=[SMEM] + [columns(start)] * 2,
        out_specs=[both(768), SMEM],
        out_shape=[shape(pairs, 2, 768, PAIR), TOKEN],
        scratch_shapes=[pltpu.VMEM((512, PAIR), F32)],
        compiler_params=vmem(LIMIT),
        name="pair_rows",
    )(role, keys, values)


def cross_rows(role, keys, values, partner, start, pairs):
    def body(role, k, v, p, near, up_out, down_out, token, spans, tmp, ours):
        even, wrap = role[0] == 0, role[1]
        odd = jnp.logical_not(even)
        pass_on(role, token)

        for which, own in ((0, k), (1, v)):
            tmp[...] = p[which].astype(F32)
            ours[...] = own[...].astype(F32)
            spans[0:128] = mean_rows(ours, 0, 128, 8)
            spans[128:160] = mean_rows(tmp, 0, 32, 8)
            spans[160:192] = mean_rows(tmp, 512, 32, 4)
            spans[192:224] = mean_rows(tmp, 640, 32, 4)
            spans[224:256] = mean_rows(tmp, 256, 32, 8)

            def theirs_down(out):
                out[which, 0:256] = p[which, 0:256]
                out[which, 256:384] = p[which, 512:640]
                out[which, 384:448] = mean_rows(tmp, 640, 64, 2)
                out[which, 448:512] = mean_rows(tmp, 256, 64, 4)

            def theirs_up(out):
                out[which, 0:256] = p[which, 256:512]
                out[which, 256:384] = p[which, 640:768]
                out[which, 384:448] = mean_rows(tmp, 0, 64, 4)
                out[which, 448:512] = mean_rows(tmp, 512, 64, 2)

            @pl.when(even)
            def _():
                theirs_down(near)
                theirs_up(up_out)
                up_out[which, 512:640] = spans[0:128]
                down_out[which, 0:256] = spans[...]

            @pl.when(odd)
            def _():
                theirs_up(near)
                theirs_down(down_out)
                down_out[which, 512:640] = spans[0:128]
                up_out[which, 0:256] = spans[...]

            @pl.when((wrap == 1) & even)
            def _():
                down_out[which, 0:256] = own[0:256]
                down_out[which, 256:384] = mean_rows(ours, 256, 128, 2)
                down_out[which, 384:512] = mean_rows(ours, 512, 128, 4)
                down_out[which, 512:640] = spans[128:256]

            @pl.when((wrap == 1) & odd)
            def _():
                up_out[which, 0:256] = own[768:1024]
                up_out[which, 256:384] = mean_rows(ours, 512, 128, 2)
                up_out[which, 384:512] = mean_rows(ours, 0, 128, 4)
                up_out[which, 512:640] = spans[128:256]

            @pl.when((wrap == 2) & even)
            def _():
                up_out[which, 0:128] = spans[128:256]
                up_out[which, 128:256] = spans[0:128]

            @pl.when((wrap == 2) & odd)
            def _():
                down_out[which, 0:128] = spans[128:256]
                down_out[which, 128:256] = spans[0:128]

    return pl.pallas_call(
        body,
        grid=(pairs,),
        in_specs=[SMEM, columns(start), columns(start), both(768)],
        out_specs=[both(512), both(640), both(640), SMEM],
        out_shape=[shape(pairs, 2, rows, PAIR) for rows in (512, 640, 640)] + [TOKEN],
        scratch_shapes=[
            pltpu.VMEM((256, PAIR), BF16), pltpu.VMEM((768, PAIR), F32), pltpu.VMEM((1024, PAIR), F32),
        ],
        compiler_params=vmem(LIMIT),
        name="cross_rows",
    )(role, keys, values, partner)


def attend(role, valid, queries, keys, values, grad_out, came, before, start, pairs):

    def side(rows, which):
        return pl.BlockSpec((None, None, rows, PAIR), lambda j: (j, which, 0, 0))

    extra = 0 if before is None else 2

    def body(*refs):
        attend_kernel(*refs[:12], *refs[12 + extra :])

    heights = (512, 640, 640)
    whole = shape(1024, queries.shape[1])
    return pl.pallas_call(
        body,
        grid=(pairs,),
        in_specs=[SMEM, SMEM] + [columns(start)] * 4
        + [side(rows, which) for rows in heights for which in (0, 1)]
        + [pl.BlockSpec(memory_space=pl.ANY)] * extra,
        out_specs=[columns(start)] * 2 + [own_rows()] * 2 + [both(rows) for rows in heights]
        + [SMEM],
        out_shape=[whole, whole]
        + [shape(pairs, 1024, PAIR, dtype=F32)] * 2
        + [shape(pairs, 2, rows, PAIR) for rows in heights]
        + [TOKEN],
        input_output_aliases={12: 0, 13: 1} if extra else {},
        scratch_shapes=[
            pltpu.VMEM((ROWS, PAIR), BF16), pltpu.VMEM((ROWS, PAIR), BF16),
            pltpu.VMEM((PAIR, ROWS), BF16), pltpu.VMEM((2, 80, ROWS), BF16),
        ]
        + [pltpu.VMEM((1920, 512), BF16)] * 2
        + [pltpu.VMEM((512, PAIR), BF16)] * 4
        + [pltpu.VMEM((ROWS, PAIR), F32)] * 2
        + [pltpu.VMEM((8, 512), F32)] * 2
        + [
            pltpu.VMEM((1024, PAIR), F32), pltpu.VMEM((768, PAIR), F32),
            pltpu.VMEM((2, 640, PAIR), BF16), pltpu.VMEM((2, 256, PAIR), BF16),
            pltpu.VMEM((2, 2, 512, PAIR), BF16),
            pltpu.SMEM((1,), jnp.int32), pltpu.SMEM((ROWS // 128,), F32),
        ],
        compiler_params=vmem(LIMIT),
        cost_estimate=pl.CostEstimate(
            flops=pairs * 14 * 10**9, bytes_accessed=pairs * 4 * 10**6, transcendentals=0
        ),
        name="attend_pairs",
    )(
        role, valid, queries, keys, values, grad_out,
        *[part for pair in came for part in (pair, pair)], *(before or ()),
    )


def pair_grads(role, near, above, below, pairs):
    def body(role, near, above, below, out, token, tmp):
        even, wrap = role[0] == 0, role[1]
        odd = jnp.logical_not(even)
        pass_on(role, token)

        def add_span(rows):
            add_rows(tmp, 0, rows[0:32], 8)
            add_rows(tmp, 512, rows[32:64], 4)
            add_rows(tmp, 640, rows[64:96], 4)
            add_rows(tmp, 256, rows[96:128], 8)

        for which in (0, 1):
            tmp[...] = jnp.zeros_like(tmp)

            @pl.when(even)
            def _():
                add_down(tmp, near[which], False)

                @pl.when(wrap != 2)
                def _():
                    add_up(tmp, above[which, 0:512], False)

                @pl.when(wrap == 2)
                def _():
                    add_span(above[which, 0:128])

                @pl.when(wrap == 1)
                def _():
                    add_span(below[which, 512:640])

                @pl.when(wrap != 1)
                def _():
                    add_span(below[which, 128:256])

            @pl.when(odd)
            def _():
                add_up(tmp, near[which], False)

                @pl.when(wrap != 2)
                def _():
                    add_down(tmp, below[which, 0:512], False)

                @pl.when(wrap == 2)
                def _():
                    add_span(below[which, 0:128])

                @pl.when(wrap == 1)
                def _():
                    add_span(above[which, 512:640])

                @pl.when(wrap != 1)
                def _():
                    add_span(above[which, 128:256])

            out[which] = tmp[...].astype(BF16)

    return pl.pallas_call(
        body,
        grid=(pairs,),
        in_specs=[SMEM, both(512), both(640), both(640)],
        out_specs=[both(768), SMEM],
        out_shape=[shape(pairs, 2, 768, PAIR), TOKEN],
        scratch_shapes=[pltpu.VMEM((768, PAIR), F32)],
        compiler_params=vmem(LIMIT),
        name="pair_grads",
    )(role, near, above, below)


def finish(role, own_k, own_v, above, below, partner, before, start, pairs):
    extra = 0 if before is None else 2

    def body(*refs):
        role, gk, gv, above, below, got = refs[:6]
        dk, dv, token, tmp = refs[6 + extra :]
        even, wrap = role[0] == 0, role[1]
        odd = jnp.logical_not(even)
        pass_on(role, token)
        for which, own, out in ((0, gk, dk), (1, gv, dv)):
            tmp[...] = own[...]
            add_rows(tmp, 0, got[which, 0:256], 1)
            add_rows(tmp, 768, got[which, 256:512], 1)
            add_rows(tmp, 256, got[which, 512:768], 2)

            for here, large, small, add in ((even, above, below, add_down), (odd, below, above, add_up)):

                @pl.when(here & (wrap != 2))
                def _():
                    add_rows(tmp, 0, large[which, 512:640], 8)

                @pl.when(here & (wrap == 2))
                def _():
                    add_rows(tmp, 0, large[which, 128:256], 8)

                @pl.when(here & (wrap != 1))
                def _():
                    add_rows(tmp, 0, small[which, 0:128], 8)

                @pl.when(here & (wrap == 1))
                def _():
                    add(tmp, small[which, 0:512], True)

            out[...] = tmp[...].astype(BF16)

    whole = shape(1024, 1024)
    return pl.pallas_call(
        body,
        grid=(pairs,),
        in_specs=[SMEM] + [own_rows()] * 2 + [both(640), both(640), both(768)]
        + [pl.BlockSpec(memory_space=pl.ANY)] * extra,
        out_specs=[columns(start)] * 2 + [SMEM],
        out_shape=[whole, whole, TOKEN],
        input_output_aliases={6: 0, 7: 1} if extra else {},
        scratch_shapes=[pltpu.VMEM((1024, PAIR), F32)],
        compiler_params=vmem(LIMIT),
        name="sum_grads",
    )(role, own_k, own_v, above, below, partner, *(before or ()))


def routes(outer, inner):
    count = outer * inner
    up = {i: i + 2 for i in range(count - 2)}
    for a in range(1, outer - 1, 2):
        last = a * inner + inner - 2
        up[last], up[last + 1] = last + 3, last + 2
    return [(i, i ^ 1) for i in range(count)], sorted(up.items())


def local(queries, keys, values, grad_out):
    a, b = lax.axis_index(AXES[0]), lax.axis_index(AXES[1])
    outer, inner = lax.axis_size(AXES[0]), lax.axis_size(AXES[1])
    index = a * inner + b
    count = outer * inner
    partners, up = routes(outer, inner)
    down = [(j, i) for i, j in up]
    above = (a % 2 == 1) & (a < outer - 1) & (b >= inner - 2)
    below = (a % 2 == 0) & (a > 0) & (b < 2)
    ends = (b == 0) | (b == inner - 1)
    odd = index % 2
    wrap = jnp.where(above | below, jnp.where(ends, 1, 2), 0)
    token = jnp.stack([odd, wrap]).astype(jnp.int32)
    sign = 1 - 2 * odd

    def there(step):
        at = index + step * sign
        return (at >= 0) & (at < count)

    valid = jnp.stack(
        [index > 0, index < count - 1, there(-2), there(2), there(3)]
    ).astype(F32)

    starts = [sum(GROUPS[:i]) for i in range(len(GROUPS))]
    partner, came, grown, near, answers, returned = {}, {}, {}, {}, {}, {}
    mixed = grads = None
    for step, i in ORDER:
        start, pairs = starts[i], GROUPS[i]
        if step == "pair":
            rows, token = pair_rows(token, keys, values, start, pairs)
            partner[i] = moved(rows, partners)
        elif step == "cross":
            side, upward, downward, token = cross_rows(
                token, keys, values, partner[i], start, pairs
            )
            came[i] = (side, moved(upward, up), moved(downward, down))
        elif step == "attend":
            *mixed, gk, gv, near[i], upward, downward, token = attend(
                token, valid, queries, keys, values, grad_out, came[i], mixed, start, pairs
            )
            grown[i] = (gk, gv)
            answers[i] = (moved(downward, down), moved(upward, up))
        elif step == "back":
            rows, token = pair_grads(token, near[i], *answers[i], pairs)
            returned[i] = moved(rows, partners)
        else:
            *grads, token = finish(token, *grown[i], *answers[i], returned[i], grads, start, pairs)
    return (*mixed, *grads)


def solution(mesh):
    placed = P(AXES, None)
    return jax.shard_map(
        local,
        mesh=mesh,
        in_specs=(placed,) * 4,
        out_specs=(placed,) * 4,
        check_vma=False,
    )
```

```python
import math

import jax
import jax.numpy as jnp
from jax import lax
from jax.experimental import pallas as pl
from jax.experimental.pallas import tpu as pltpu
from jax.sharding import PartitionSpec as P

HEAD_DIM = 64
BLOCK = 256
HALF = 128
PAIR = 128
AXES = ("seqa", "seqb")
GROUPS = (2, 3, 2, 1)
ORDER = (
    ("pair", 0), ("cross", 0), ("pair", 1),
    ("attend", 0), ("cross", 1), ("pair", 2), ("cross", 2), ("pair", 3),
    ("attend", 1), ("cross", 3), ("back", 0),
    ("attend", 2), ("back", 1),
    ("attend", 3), ("back", 2), ("sum", 0), ("back", 3), ("sum", 1), ("sum", 2), ("sum", 3),
)
LIMIT = 60
LOG2E = math.log2(math.e)
BF16 = jnp.bfloat16
F32 = jnp.float32
NT = (((1,), (1,)), ((), ()))
NN = (((1,), (0,)), ((), ()))

BASE = (0, 1536, 2560, 3072)
ROWS = 3456

PIECES = ((768, 0), (384, 768), (384, 1152), (384, 1536))


def piece_starts(b):
    half = b // 2
    first = BASE[1] + half * 512 + (1 - (b - 2 * half)) * 128
    rows = (b * 256, first, BASE[2] + half * 128, BASE[3])
    return [r if isinstance(r, int) else pl.multiple_of(r, 128) for r in rows]


def dot(a, b, dims=NN):
    return lax.dot_general(a, b, dims, preferred_element_type=F32)


def mean_rows(ref, start, count, stride):
    total = ref[pl.ds(start, count, stride=stride), :]
    for i in range(1, stride):
        total = total + ref[pl.ds(start + i, count, stride=stride), :]
    return (total * (1.0 / stride)).astype(BF16)


def add_rows(ref, start, rows, stride):
    if stride == 1:
        at = slice(start, start + rows.shape[0])
        ref[at] = ref[at] + rows.astype(F32)
    else:
        spread_rows(ref, start, rows.astype(F32), stride)


def spread_rows(ref, start, rows, stride):
    for i in range(stride):
        at = pl.ds(start + i, rows.shape[0], stride=stride)
        ref[at, :] = ref[at, :] + rows


def attend_kernel(
    role, valid, q, k, v, do, hk, hv, bk, bv, ak, av,
    o, dq, gk, gv, rh, rup, rdown, token,
    kext, vext, kt, vt, e, x, qz, doz, qs, dos, acck, accv, inn, rls, ftmp, gtmp,
    cross, small, side, flag, oks,
):
    lane = lax.broadcasted_iota(jnp.int32, (256, PAIR), 1)
    first = lane < HEAD_DIM
    even = role[0] == 0
    odd = jnp.logical_not(even)
    pass_on(role, token)

    for which, (h, b, a) in enumerate(((hk, bk, ak), (hv, bv, av))):

        @pl.when(even)
        def _():
            cross[which] = b[...]
            small[which] = a[0:256]
            side[0, which] = b[0:512]
            side[1, which] = h[...]

        @pl.when(odd)
        def _():
            cross[which] = a[...]
            small[which] = b[0:256]
            side[0, which] = h[...]
            side[1, which] = a[0:512]

    for which, own, ext in ((0, k, kext), (1, v, vext)):
        low, up = side.at[0, which], side.at[1, which]
        ext[0:256] = low[0:256]
        ext[256:1280] = own[...]
        ext[1280:1536] = up[0:256]
        ftmp[...] = own[...].astype(F32)
        spans = mean_rows(ftmp, 0, 512, 2)
        b1 = BASE[1]
        ext[b1 + 256 : b1 + 384] = spans[384:512]
        ext[b1 + 384 : b1 + 512] = spans[256:384]
        ext[b1 + 512 : b1 + 640] = spans[128:256]
        ext[b1 + 640 : b1 + 768] = spans[0:128]
        ext[b1 + 128 : b1 + 256] = low[256:384]
        ext[b1 + 768 : b1 + 896] = up[256:384]
        b2 = BASE[2]
        ftmp[0:384] = low[0:384].astype(F32)
        ext[b1 : b1 + 128] = mean_rows(ftmp, 0, 128, 2)
        ext[b2 + 384 : b2 + 448] = mean_rows(ftmp, 256, 64, 2)
        ext[b2 + 448 : b2 + 512] = mean_rows(ftmp, 0, 64, 4)
        ftmp[0:384] = up[0:384].astype(F32)
        ext[b1 + 896 : b1 + 1024] = mean_rows(ftmp, 0, 128, 2)
        ext[b2 : b2 + 64] = mean_rows(ftmp, 0, 64, 4)
        ext[b2 + 64 : b2 + 128] = mean_rows(ftmp, 256, 64, 2)
        ext[b2 + 128 : b2 + 256] = low[384:512]
        ext[b2 + 256 : b2 + 384] = up[384:512]
        ext[BASE[3] : BASE[3] + 128] = cross[which, 512:640]
        ext[BASE[3] + 128 : ROWS] = small[which]

    low_ok, up_ok = valid[0], valid[1]
    for level, row, rows, ok in (
        (0, 0, 256, low_ok), (0, 256, 1024, 1.0), (0, 1280, 256, up_ok),
        (1, 0, 256, low_ok), (1, 256, 512, 1.0), (1, 768, 256, up_ok),
        (2, 0, 128, up_ok), (2, 128, 128, low_ok), (2, 256, 128, up_ok), (2, 384, 128, low_ok),
        (3, 0, 128, valid[2]), (3, 128, 128, valid[3]), (3, 256, 128, valid[4]),
    ):
        at = slice(BASE[level] + row, BASE[level] + row + rows)
        for i in range(at.start // 128, at.stop // 128):
            oks[i] = ok
        scale = float(2**level)
        kt[:, at] = (kext[at] * scale).astype(BF16).T
        vals = (vext[at] * scale).astype(BF16).T
        top = lax.broadcasted_iota(jnp.int32, (16, rows), 0) == 0
        ones = jnp.where(top, ok * scale, 0.0).astype(BF16)
        for h in range(2):
            vt[h, 0:64, at] = vals[h * 64 : h * 64 + 64]
            vt[h, 64:80, at] = ones

    acck[...] = jnp.zeros_like(acck)
    accv[...] = jnp.zeros_like(accv)

    def block_step(b, carry):
        at = pl.ds(pl.multiple_of(b * 256, 256), 256)
        starts = piece_starts(b)
        spots = [(pl.ds(r, n), slice(to, to + n)) for r, (n, to) in zip(starts, PIECES)]
        query, grad = q[at].astype(F32), do[at].astype(F32)
        heads = (slice(0, 256), slice(256, 512))
        for h in range(2):
            mine = first if h == 0 else ~first
            qz[heads[h]] = jnp.where(mine, query * 0.125, 0.0).astype(BF16)
            doz[heads[h]] = jnp.where(mine, grad, 0.0).astype(BF16)

        for rows, to in spots:
            for h in heads:
                s = dot(kext[rows], qz[h], NT)
                e[to, h] = jnp.exp2(s * LOG2E).astype(BF16)

        def forward():
            outs, recips = [], []
            least, most = None, None
            for h in range(2):
                acc = jnp.zeros((80, 256), F32)
                for rows, to in spots:
                    acc = acc + dot(vt[h, :, rows], e[to, heads[h]])
                total = acc[64:65]
                least = total if least is None else jnp.minimum(least, total)
                most = total if most is None else jnp.maximum(most, total)
                recip = 1.0 / total
                outs.append(acc[0:64] * recip)
                recips.append(recip)
            fine = (jnp.min(least) > 2.0**-60) & (jnp.max(most) < 2.0**60)
            flag[0] = jnp.where(fine, 0, 1)
            return outs, recips

        def settle(outs, recips):
            mixed = jnp.concatenate(outs, 0)
            o[at] = mixed.T.astype(BF16)
            prod = mixed.astype(BF16).astype(F32) * grad.T
            wide = jnp.concatenate([jnp.broadcast_to(r, (64, 256)) for r in recips], 0).T
            for h in range(2):
                inn[0:1, heads[h]] = jnp.sum(prod[h * 64 : h * 64 + 64], axis=0, keepdims=True)
                rls[0:1, heads[h]] = recips[h]
                mine = first if h == 0 else ~first
                dos[heads[h]] = jnp.where(mine, grad * wide, 0.0).astype(BF16)
                qs[heads[h]] = jnp.where(mine, query * (wide * 0.125), 0.0).astype(BF16)

        settle(*forward())

        @pl.when(flag[0] == 1)
        def _():
            for h in heads:

                def scores(row):
                    row = pl.multiple_of(row, 128)
                    s = dot(kext[pl.ds(row, 128)], qz[h], NT) * LOG2E
                    return jnp.where(oks[row // 128] > 0.5, s, -jnp.inf)

                highest = jnp.full((1, 256), -jnp.inf, F32)
                for r, (n, to) in zip(starts, PIECES):
                    highest = lax.fori_loop(
                        0,
                        n // 128,
                        lambda t, top: jnp.maximum(
                            top, jnp.max(scores(r + t * 128), axis=0, keepdims=True)
                        ),
                        highest,
                    )
                for r, (n, to) in zip(starts, PIECES):

                    def again(t, carry):
                        put = pl.ds(pl.multiple_of(to + t * 128, 128), 128)
                        e[put, h] = jnp.exp2(scores(r + t * 128) - highest).astype(BF16)
                        return carry

                    lax.fori_loop(0, n // 128, again, 0)
            settle(*forward())

        for rows, to in spots:
            for h in heads:
                dp = dot(vext[rows], doz[h], NT) - inn[0:1, h]
                x[to, h] = e[to, h] * dp.astype(BF16)

        outs = []
        for h in range(2):
            acc = jnp.zeros((64, 256), F32)
            for rows, to in spots:
                acc = acc + dot(kt[h * 64 : h * 64 + 64, rows], x[to, heads[h]])
            outs.append(acc * (rls[0:1, heads[h]] * 0.125))
        dq[at] = jnp.concatenate(outs, 0).T.astype(BF16)

        for rows, to in spots:
            acck[rows] = acck[rows] + dot(x[to], qs[...])
            accv[rows] = accv[rows] + dot(e[to], dos[...])
        return carry

    lax.fori_loop(0, 4, block_step, 0)

    b1, b2, b3 = BASE[1:]
    for which, acc, own in ((0, acck, gk), (1, accv, gv)):
        low, up = side.at[0, which], side.at[1, which]
        own[...] = acc[256:1280]
        for i, row in enumerate((640, 512, 384, 256)):
            spread_rows(own, i * 256, acc[b1 + row : b1 + row + 128], 2)
        gtmp[0:256] = acc[0:256]
        spread_rows(gtmp, 0, acc[b1 : b1 + 128], 2)
        spread_rows(gtmp, 0, acc[b2 + 448 : b2 + 512], 4)
        gtmp[256:384] = acc[b1 + 128 : b1 + 256]
        spread_rows(gtmp, 256, acc[b2 + 384 : b2 + 448], 2)
        gtmp[384:640] = acc[1280:1536]
        spread_rows(gtmp, 384, acc[b1 + 896 : b1 + 1024], 2)
        spread_rows(gtmp, 384, acc[b2 : b2 + 64], 4)
        gtmp[640:768] = acc[b1 + 768 : b1 + 896]
        spread_rows(gtmp, 640, acc[b2 + 64 : b2 + 128], 2)
        low[0:384] = gtmp[0:384].astype(BF16)
        up[0:384] = gtmp[384:768].astype(BF16)
        low[384:512] = acc[b2 + 128 : b2 + 256].astype(BF16)
        up[384:512] = acc[b2 + 256 : b2 + 384].astype(BF16)
        cross[which, 512:640] = acc[b3 : b3 + 128].astype(BF16)
        small[which] = acc[b3 + 128 : ROWS].astype(BF16)

        @pl.when(even)
        def _():
            rh[which] = up[...]
            rdown[which, 0:512] = low[...]
            rdown[which, 512:640] = cross[which, 512:640]
            rup[which, 0:256] = small[which]

        @pl.when(odd)
        def _():
            rh[which] = low[...]
            rup[which, 0:512] = up[...]
            rup[which, 512:640] = cross[which, 512:640]
            rdown[which, 0:256] = small[which]


def pass_on(role, token):
    token[0] = role[0]
    token[1] = role[1]


def add_down(ref, rows, own):
    add_rows(ref, 0, rows[0:256], 1)
    if own:
        add_rows(ref, 256, rows[256:384], 2)
        add_rows(ref, 512, rows[384:512], 4)
    else:
        add_rows(ref, 512, rows[256:384], 1)
        add_rows(ref, 640, rows[384:448], 2)
        add_rows(ref, 256, rows[448:512], 4)


def add_up(ref, rows, own):
    if own:
        add_rows(ref, 768, rows[0:256], 1)
        add_rows(ref, 512, rows[256:384], 2)
        add_rows(ref, 0, rows[384:512], 4)
    else:
        add_rows(ref, 256, rows[0:256], 1)
        add_rows(ref, 640, rows[256:384], 1)
        add_rows(ref, 0, rows[384:448], 4)
        add_rows(ref, 512, rows[448:512], 2)


def moved(array, pairs):
    return lax.ppermute(array, AXES, pairs)


def shape(*dims, dtype=BF16):
    return jax.ShapeDtypeStruct(dims, dtype)


def vmem(limit):
    return pltpu.CompilerParams(vmem_limit_bytes=limit * 2**20)


SMEM = pl.BlockSpec(memory_space=pltpu.SMEM)


def both(rows):
    return pl.BlockSpec((None, 2, rows, PAIR), lambda j: (j, 0, 0, 0))


def own_rows():
    return pl.BlockSpec((None, 1024, PAIR), lambda j: (j, 0, 0))


def columns(start):
    return pl.BlockSpec((1024, PAIR), lambda j: (0, start + j))


TOKEN = shape(2, dtype=jnp.int32)


def pair_rows(role, keys, values, start, pairs):
    def body(role, k, v, out, token, tmp):
        pass_on(role, token)
        for which, own in ((0, k), (1, v)):
            tmp[...] = own[256:768].astype(F32)
            out[which, 0:256] = own[0:256]
            out[which, 256:512] = own[768:1024]
            out[which, 512:768] = mean_rows(tmp, 0, 256, 2)

    return pl.pallas_call(
        body,
        grid=(pairs,),
        in_specs=[SMEM] + [columns(start)] * 2,
        out_specs=[both(768), SMEM],
        out_shape=[shape(pairs, 2, 768, PAIR), TOKEN],
        scratch_shapes=[pltpu.VMEM((512, PAIR), F32)],
        compiler_params=vmem(LIMIT),
        name="pair_rows",
    )(role, keys, values)


def cross_rows(role, keys, values, partner, start, pairs):
    def body(role, k, v, p, near, up_out, down_out, token, spans, tmp, ours):
        even, wrap = role[0] == 0, role[1]
        odd = jnp.logical_not(even)
        pass_on(role, token)

        for which, own in ((0, k), (1, v)):
            tmp[...] = p[which].astype(F32)
            ours[...] = own[...].astype(F32)
            spans[0:128] = mean_rows(ours, 0, 128, 8)
            spans[128:160] = mean_rows(tmp, 0, 32, 8)
            spans[160:192] = mean_rows(tmp, 512, 32, 4)
            spans[192:224] = mean_rows(tmp, 640, 32, 4)
            spans[224:256] = mean_rows(tmp, 256, 32, 8)

            def theirs_down(out):
                out[which, 0:256] = p[which, 0:256]
                out[which, 256:384] = p[which, 512:640]
                out[which, 384:448] = mean_rows(tmp, 640, 64, 2)
                out[which, 448:512] = mean_rows(tmp, 256, 64, 4)

            def theirs_up(out):
                out[which, 0:256] = p[which, 256:512]
                out[which, 256:384] = p[which, 640:768]
                out[which, 384:448] = mean_rows(tmp, 0, 64, 4)
                out[which, 448:512] = mean_rows(tmp, 512, 64, 2)

            @pl.when(even)
            def _():
                theirs_down(near)
                theirs_up(up_out)
                up_out[which, 512:640] = spans[0:128]
                down_out[which, 0:256] = spans[...]

            @pl.when(odd)
            def _():
                theirs_up(near)
                theirs_down(down_out)
                down_out[which, 512:640] = spans[0:128]
                up_out[which, 0:256] = spans[...]

            @pl.when((wrap == 1) & even)
            def _():
                down_out[which, 0:256] = own[0:256]
                down_out[which, 256:384] = mean_rows(ours, 256, 128, 2)
                down_out[which, 384:512] = mean_rows(ours, 512, 128, 4)
                down_out[which, 512:640] = spans[128:256]

            @pl.when((wrap == 1) & odd)
            def _():
                up_out[which, 0:256] = own[768:1024]
                up_out[which, 256:384] = mean_rows(ours, 512, 128, 2)
                up_out[which, 384:512] = mean_rows(ours, 0, 128, 4)
                up_out[which, 512:640] = spans[128:256]

            @pl.when((wrap == 2) & even)
            def _():
                up_out[which, 0:128] = spans[128:256]
                up_out[which, 128:256] = spans[0:128]

            @pl.when((wrap == 2) & odd)
            def _():
                down_out[which, 0:128] = spans[128:256]
                down_out[which, 128:256] = spans[0:128]

    return pl.pallas_call(
        body,
        grid=(pairs,),
        in_specs=[SMEM, columns(start), columns(start), both(768)],
        out_specs=[both(512), both(640), both(640), SMEM],
        out_shape=[shape(pairs, 2, rows, PAIR) for rows in (512, 640, 640)] + [TOKEN],
        scratch_shapes=[
            pltpu.VMEM((256, PAIR), BF16), pltpu.VMEM((768, PAIR), F32), pltpu.VMEM((1024, PAIR), F32),
        ],
        compiler_params=vmem(LIMIT),
        name="cross_rows",
    )(role, keys, values, partner)


def attend(role, valid, queries, keys, values, grad_out, came, before, start, pairs):

    def side(rows, which):
        return pl.BlockSpec((None, None, rows, PAIR), lambda j: (j, which, 0, 0))

    extra = 0 if before is None else 2

    def body(*refs):
        attend_kernel(*refs[:12], *refs[12 + extra :])

    heights = (512, 640, 640)
    whole = shape(1024, queries.shape[1])
    return pl.pallas_call(
        body,
        grid=(pairs,),
        in_specs=[SMEM, SMEM] + [columns(start)] * 4
        + [side(rows, which) for rows in heights for which in (0, 1)]
        + [pl.BlockSpec(memory_space=pl.ANY)] * extra,
        out_specs=[columns(start)] * 2 + [own_rows()] * 2 + [both(rows) for rows in heights]
        + [SMEM],
        out_shape=[whole, whole]
        + [shape(pairs, 1024, PAIR, dtype=F32)] * 2
        + [shape(pairs, 2, rows, PAIR) for rows in heights]
        + [TOKEN],
        input_output_aliases={12: 0, 13: 1} if extra else {},
        scratch_shapes=[
            pltpu.VMEM((ROWS, PAIR), BF16), pltpu.VMEM((ROWS, PAIR), BF16),
            pltpu.VMEM((PAIR, ROWS), BF16), pltpu.VMEM((2, 80, ROWS), BF16),
        ]
        + [pltpu.VMEM((1920, 512), BF16)] * 2
        + [pltpu.VMEM((512, PAIR), BF16)] * 4
        + [pltpu.VMEM((ROWS, PAIR), F32)] * 2
        + [pltpu.VMEM((8, 512), F32)] * 2
        + [
            pltpu.VMEM((1024, PAIR), F32), pltpu.VMEM((768, PAIR), F32),
            pltpu.VMEM((2, 640, PAIR), BF16), pltpu.VMEM((2, 256, PAIR), BF16),
            pltpu.VMEM((2, 2, 512, PAIR), BF16),
            pltpu.SMEM((1,), jnp.int32), pltpu.SMEM((ROWS // 128,), F32),
        ],
        compiler_params=vmem(LIMIT),
        cost_estimate=pl.CostEstimate(
            flops=pairs * 14 * 10**9, bytes_accessed=pairs * 4 * 10**6, transcendentals=0
        ),
        name="attend_pairs",
    )(
        role, valid, queries, keys, values, grad_out,
        *[part for pair in came for part in (pair, pair)], *(before or ()),
    )


def pair_grads(role, near, above, below, pairs):
    def body(role, near, above, below, out, token, tmp):
        even, wrap = role[0] == 0, role[1]
        odd = jnp.logical_not(even)
        pass_on(role, token)

        def add_span(rows):
            add_rows(tmp, 0, rows[0:32], 8)
            add_rows(tmp, 512, rows[32:64], 4)
            add_rows(tmp, 640, rows[64:96], 4)
            add_rows(tmp, 256, rows[96:128], 8)

        for which in (0, 1):
            tmp[...] = jnp.zeros_like(tmp)

            @pl.when(even)
            def _():
                add_down(tmp, near[which], False)

                @pl.when(wrap != 2)
                def _():
                    add_up(tmp, above[which, 0:512], False)

                @pl.when(wrap == 2)
                def _():
                    add_span(above[which, 0:128])

                @pl.when(wrap == 1)
                def _():
                    add_span(below[which, 512:640])

                @pl.when(wrap != 1)
                def _():
                    add_span(below[which, 128:256])

            @pl.when(odd)
            def _():
                add_up(tmp, near[which], False)

                @pl.when(wrap != 2)
                def _():
                    add_down(tmp, below[which, 0:512], False)

                @pl.when(wrap == 2)
                def _():
                    add_span(below[which, 0:128])

                @pl.when(wrap == 1)
                def _():
                    add_span(above[which, 512:640])

                @pl.when(wrap != 1)
                def _():
                    add_span(above[which, 128:256])

            out[which] = tmp[...].astype(BF16)

    return pl.pallas_call(
        body,
        grid=(pairs,),
        in_specs=[SMEM, both(512), both(640), both(640)],
        out_specs=[both(768), SMEM],
        out_shape=[shape(pairs, 2, 768, PAIR), TOKEN],
        scratch_shapes=[pltpu.VMEM((768, PAIR), F32)],
        compiler_params=vmem(LIMIT),
        name="pair_grads",
    )(role, near, above, below)


def finish(role, own_k, own_v, above, below, partner, before, start, pairs):
    extra = 0 if before is None else 2

    def body(*refs):
        role, gk, gv, above, below, got = refs[:6]
        dk, dv, token, tmp = refs[6 + extra :]
        even, wrap = role[0] == 0, role[1]
        odd = jnp.logical_not(even)
        pass_on(role, token)
        for which, own, out in ((0, gk, dk), (1, gv, dv)):
            tmp[...] = own[...]
            add_rows(tmp, 0, got[which, 0:256], 1)
            add_rows(tmp, 768, got[which, 256:512], 1)
            add_rows(tmp, 256, got[which, 512:768], 2)

            for here, large, small, add in ((even, above, below, add_down), (odd, below, above, add_up)):

                @pl.when(here & (wrap != 2))
                def _():
                    add_rows(tmp, 0, large[which, 512:640], 8)

                @pl.when(here & (wrap == 2))
                def _():
                    add_rows(tmp, 0, large[which, 128:256], 8)

                @pl.when(here & (wrap != 1))
                def _():
                    add_rows(tmp, 0, small[which, 0:128], 8)

                @pl.when(here & (wrap == 1))
                def _():
                    add(tmp, small[which, 0:512], True)

            out[...] = tmp[...].astype(BF16)

    whole = shape(1024, 1024)
    return pl.pallas_call(
        body,
        grid=(pairs,),
        in_specs=[SMEM] + [own_rows()] * 2 + [both(640), both(640), both(768)]
        + [pl.BlockSpec(memory_space=pl.ANY)] * extra,
        out_specs=[columns(start)] * 2 + [SMEM],
        out_shape=[whole, whole, TOKEN],
        input_output_aliases={6: 0, 7: 1} if extra else {},
        scratch_shapes=[pltpu.VMEM((1024, PAIR), F32)],
        compiler_params=vmem(LIMIT),
        name="sum_grads",
    )(role, own_k, own_v, above, below, partner, *(before or ()))


def routes(outer, inner):
    count = outer * inner
    up = {i: i + 2 for i in range(count - 2)}
    for a in range(1, outer - 1, 2):
        last = a * inner + inner - 2
        up[last], up[last + 1] = last + 3, last + 2
    return [(i, i ^ 1) for i in range(count)], sorted(up.items())


def local(queries, keys, values, grad_out):
    a, b = lax.axis_index(AXES[0]), lax.axis_index(AXES[1])
    outer, inner = lax.axis_size(AXES[0]), lax.axis_size(AXES[1])
    index = a * inner + b
    count = outer * inner
    partners, up = routes(outer, inner)
    down = [(j, i) for i, j in up]
    above = (a % 2 == 1) & (a < outer - 1) & (b >= inner - 2)
    below = (a % 2 == 0) & (a > 0) & (b < 2)
    ends = (b == 0) | (b == inner - 1)
    odd = index % 2
    wrap = jnp.where(above | below, jnp.where(ends, 1, 2), 0)
    token = jnp.stack([odd, wrap]).astype(jnp.int32)
    sign = 1 - 2 * odd

    def there(step):
        at = index + step * sign
        return (at >= 0) & (at < count)

    valid = jnp.stack(
        [index > 0, index < count - 1, there(-2), there(2), there(3)]
    ).astype(F32)

    starts = [sum(GROUPS[:i]) for i in range(len(GROUPS))]
    partner, came, grown, near, answers, returned = {}, {}, {}, {}, {}, {}
    mixed = grads = None
    for step, i in ORDER:
        start, pairs = starts[i], GROUPS[i]
        if step == "pair":
            rows, token = pair_rows(token, keys, values, start, pairs)
            partner[i] = moved(rows, partners)
        elif step == "cross":
            side, upward, downward, token = cross_rows(
                token, keys, values, partner[i], start, pairs
            )
            came[i] = (side, moved(upward, up), moved(downward, down))
        elif step == "attend":
            *mixed, gk, gv, near[i], upward, downward, token = attend(
                token, valid, queries, keys, values, grad_out, came[i], mixed, start, pairs
            )
            grown[i] = (gk, gv)
            answers[i] = (moved(downward, down), moved(upward, up))
        elif step == "back":
            rows, token = pair_grads(token, near[i], *answers[i], pairs)
            returned[i] = moved(rows, partners)
        else:
            *grads, token = finish(token, *grown[i], *answers[i], returned[i], grads, start, pairs)
    return (*mixed, *grads)


def solution(mesh):
    placed = P(AXES, None)
    return jax.shard_map(
        local,
        mesh=mesh,
        in_specs=(placed,) * 4,
        out_specs=(placed,) * 4,
        check_vma=False,
    )
```

```python
import math

import jax
import jax.numpy as jnp
from jax import lax
from jax.experimental import pallas as pl
from jax.experimental.pallas import tpu as pltpu
from jax.sharding import PartitionSpec as P

HEAD_DIM = 64
BLOCK = 256
HALF = 128
PAIR = 128
AXES = ("seqa", "seqb")
GROUPS = (2, 3, 2, 1)
ORDER = (
    ("pair", 0), ("cross", 0), ("pair", 1),
    ("attend", 0), ("cross", 1), ("pair", 2), ("pair", 3),
    ("attend", 1), ("cross", 2), ("cross", 3), ("back", 0),
    ("attend", 2), ("back", 1),
    ("attend", 3), ("back", 2), ("sum", 0), ("back", 3), ("sum", 1), ("sum", 2), ("sum", 3),
)
LIMIT = 60
LOG2E = math.log2(math.e)
BF16 = jnp.bfloat16
F32 = jnp.float32
NT = (((1,), (1,)), ((), ()))
NN = (((1,), (0,)), ((), ()))

BASE = (0, 1536, 2560, 3072)
ROWS = 3456

PIECES = ((768, 0), (384, 768), (384, 1152), (384, 1536))


def piece_starts(b):
    half = b // 2
    first = BASE[1] + half * 512 + (1 - (b - 2 * half)) * 128
    rows = (b * 256, first, BASE[2] + half * 128, BASE[3])
    return [r if isinstance(r, int) else pl.multiple_of(r, 128) for r in rows]


def dot(a, b, dims=NN):
    return lax.dot_general(a, b, dims, preferred_element_type=F32)


def mean_rows(ref, start, count, stride):
    total = ref[pl.ds(start, count, stride=stride), :]
    for i in range(1, stride):
        total = total + ref[pl.ds(start + i, count, stride=stride), :]
    return (total * (1.0 / stride)).astype(BF16)


def add_rows(ref, start, rows, stride):
    if stride == 1:
        at = slice(start, start + rows.shape[0])
        ref[at] = ref[at] + rows.astype(F32)
    else:
        spread_rows(ref, start, rows.astype(F32), stride)


def spread_rows(ref, start, rows, stride):
    for i in range(stride):
        at = pl.ds(start + i, rows.shape[0], stride=stride)
        ref[at, :] = ref[at, :] + rows


def attend_kernel(
    role, valid, q, k, v, do, hk, hv, bk, bv, ak, av,
    o, dq, gk, gv, rh, rup, rdown, token,
    kext, vext, kt, vt, e, x, qz, doz, qs, dos, acck, accv, inn, rls, ftmp, gtmp,
    cross, small, side, flag, oks,
):
    lane = lax.broadcasted_iota(jnp.int32, (256, PAIR), 1)
    first = lane < HEAD_DIM
    even = role[0] == 0
    odd = jnp.logical_not(even)
    pass_on(role, token)

    for which, (h, b, a) in enumerate(((hk, bk, ak), (hv, bv, av))):

        @pl.when(even)
        def _():
            cross[which] = b[...]
            small[which] = a[0:256]
            side[0, which] = b[0:512]
            side[1, which] = h[...]

        @pl.when(odd)
        def _():
            cross[which] = a[...]
            small[which] = b[0:256]
            side[0, which] = h[...]
            side[1, which] = a[0:512]

    for which, own, ext in ((0, k, kext), (1, v, vext)):
        low, up = side.at[0, which], side.at[1, which]
        ext[0:256] = low[0:256]
        ext[256:1280] = own[...]
        ext[1280:1536] = up[0:256]
        ftmp[...] = own[...].astype(F32)
        spans = mean_rows(ftmp, 0, 512, 2)
        b1 = BASE[1]
        ext[b1 + 256 : b1 + 384] = spans[384:512]
        ext[b1 + 384 : b1 + 512] = spans[256:384]
        ext[b1 + 512 : b1 + 640] = spans[128:256]
        ext[b1 + 640 : b1 + 768] = spans[0:128]
        ext[b1 + 128 : b1 + 256] = low[256:384]
        ext[b1 + 768 : b1 + 896] = up[256:384]
        b2 = BASE[2]
        ftmp[0:384] = low[0:384].astype(F32)
        ext[b1 : b1 + 128] = mean_rows(ftmp, 0, 128, 2)
        ext[b2 + 384 : b2 + 448] = mean_rows(ftmp, 256, 64, 2)
        ext[b2 + 448 : b2 + 512] = mean_rows(ftmp, 0, 64, 4)
        ftmp[0:384] = up[0:384].astype(F32)
        ext[b1 + 896 : b1 + 1024] = mean_rows(ftmp, 0, 128, 2)
        ext[b2 : b2 + 64] = mean_rows(ftmp, 0, 64, 4)
        ext[b2 + 64 : b2 + 128] = mean_rows(ftmp, 256, 64, 2)
        ext[b2 + 128 : b2 + 256] = low[384:512]
        ext[b2 + 256 : b2 + 384] = up[384:512]
        ext[BASE[3] : BASE[3] + 128] = cross[which, 512:640]
        ext[BASE[3] + 128 : ROWS] = small[which]

    low_ok, up_ok = valid[0], valid[1]
    for level, row, rows, ok in (
        (0, 0, 256, low_ok), (0, 256, 1024, 1.0), (0, 1280, 256, up_ok),
        (1, 0, 256, low_ok), (1, 256, 512, 1.0), (1, 768, 256, up_ok),
        (2, 0, 128, up_ok), (2, 128, 128, low_ok), (2, 256, 128, up_ok), (2, 384, 128, low_ok),
        (3, 0, 128, valid[2]), (3, 128, 128, valid[3]), (3, 256, 128, valid[4]),
    ):
        at = slice(BASE[level] + row, BASE[level] + row + rows)
        for i in range(at.start // 128, at.stop // 128):
            oks[i] = ok
        scale = float(2**level)
        kt[:, at] = (kext[at] * scale).astype(BF16).T
        vals = (vext[at] * scale).astype(BF16).T
        top = lax.broadcasted_iota(jnp.int32, (16, rows), 0) == 0
        ones = jnp.where(top, ok * scale, 0.0).astype(BF16)
        for h in range(2):
            vt[h, 0:64, at] = vals[h * 64 : h * 64 + 64]
            vt[h, 64:80, at] = ones

    acck[...] = jnp.zeros_like(acck)
    accv[...] = jnp.zeros_like(accv)

    def block_step(b, carry):
        at = pl.ds(pl.multiple_of(b * 256, 256), 256)
        starts = piece_starts(b)
        spots = [(pl.ds(r, n), slice(to, to + n)) for r, (n, to) in zip(starts, PIECES)]
        query, grad = q[at].astype(F32), do[at].astype(F32)
        heads = (slice(0, 256), slice(256, 512))
        for h in range(2):
            mine = first if h == 0 else ~first
            qz[heads[h]] = jnp.where(mine, query * 0.125, 0.0).astype(BF16)
            doz[heads[h]] = jnp.where(mine, grad, 0.0).astype(BF16)

        for rows, to in spots:
            for h in heads:
                s = dot(kext[rows], qz[h], NT)
                e[to, h] = jnp.exp2(s * LOG2E).astype(BF16)

        def forward():
            outs, recips = [], []
            least, most = None, None
            for h in range(2):
                acc = jnp.zeros((80, 256), F32)
                for rows, to in spots:
                    acc = acc + dot(vt[h, :, rows], e[to, heads[h]])
                total = acc[64:65]
                least = total if least is None else jnp.minimum(least, total)
                most = total if most is None else jnp.maximum(most, total)
                recip = 1.0 / total
                outs.append(acc[0:64] * recip)
                recips.append(recip)
            fine = (jnp.min(least) > 2.0**-60) & (jnp.max(most) < 2.0**60)
            flag[0] = jnp.where(fine, 0, 1)
            return outs, recips

        def settle(outs, recips):
            mixed = jnp.concatenate(outs, 0)
            o[at] = mixed.T.astype(BF16)
            prod = mixed.astype(BF16).astype(F32) * grad.T
            wide = jnp.concatenate([jnp.broadcast_to(r, (64, 256)) for r in recips], 0).T
            for h in range(2):
                inn[0:1, heads[h]] = jnp.sum(prod[h * 64 : h * 64 + 64], axis=0, keepdims=True)
                rls[0:1, heads[h]] = recips[h]
                mine = first if h == 0 else ~first
                dos[heads[h]] = jnp.where(mine, grad * wide, 0.0).astype(BF16)
                qs[heads[h]] = jnp.where(mine, query * (wide * 0.125), 0.0).astype(BF16)

        settle(*forward())

        @pl.when(flag[0] == 1)
        def _():
            for h in heads:

                def scores(row):
                    row = pl.multiple_of(row, 128)
                    s = dot(kext[pl.ds(row, 128)], qz[h], NT) * LOG2E
                    return jnp.where(oks[row // 128] > 0.5, s, -jnp.inf)

                highest = jnp.full((1, 256), -jnp.inf, F32)
                for r, (n, to) in zip(starts, PIECES):
                    highest = lax.fori_loop(
                        0,
                        n // 128,
                        lambda t, top: jnp.maximum(
                            top, jnp.max(scores(r + t * 128), axis=0, keepdims=True)
                        ),
                        highest,
                    )
                for r, (n, to) in zip(starts, PIECES):

                    def again(t, carry):
                        put = pl.ds(pl.multiple_of(to + t * 128, 128), 128)
                        e[put, h] = jnp.exp2(scores(r + t * 128) - highest).astype(BF16)
                        return carry

                    lax.fori_loop(0, n // 128, again, 0)
            settle(*forward())

        for rows, to in spots:
            for h in heads:
                dp = dot(vext[rows], doz[h], NT) - inn[0:1, h]
                x[to, h] = e[to, h] * dp.astype(BF16)

        outs = []
        for h in range(2):
            acc = jnp.zeros((64, 256), F32)
            for rows, to in spots:
                acc = acc + dot(kt[h * 64 : h * 64 + 64, rows], x[to, heads[h]])
            outs.append(acc * (rls[0:1, heads[h]] * 0.125))
        dq[at] = jnp.concatenate(outs, 0).T.astype(BF16)

        for rows, to in spots:
            acck[rows] = acck[rows] + dot(x[to], qs[...])
            accv[rows] = accv[rows] + dot(e[to], dos[...])
        return carry

    lax.fori_loop(0, 4, block_step, 0)

    b1, b2, b3 = BASE[1:]
    for which, acc, own in ((0, acck, gk), (1, accv, gv)):
        low, up = side.at[0, which], side.at[1, which]
        own[...] = acc[256:1280]
        for i, row in enumerate((640, 512, 384, 256)):
            spread_rows(own, i * 256, acc[b1 + row : b1 + row + 128], 2)
        gtmp[0:256] = acc[0:256]
        spread_rows(gtmp, 0, acc[b1 : b1 + 128], 2)
        spread_rows(gtmp, 0, acc[b2 + 448 : b2 + 512], 4)
        gtmp[256:384] = acc[b1 + 128 : b1 + 256]
        spread_rows(gtmp, 256, acc[b2 + 384 : b2 + 448], 2)
        gtmp[384:640] = acc[1280:1536]
        spread_rows(gtmp, 384, acc[b1 + 896 : b1 + 1024], 2)
        spread_rows(gtmp, 384, acc[b2 : b2 + 64], 4)
        gtmp[640:768] = acc[b1 + 768 : b1 + 896]
        spread_rows(gtmp, 640, acc[b2 + 64 : b2 + 128], 2)
        low[0:384] = gtmp[0:384].astype(BF16)
        up[0:384] = gtmp[384:768].astype(BF16)
        low[384:512] = acc[b2 + 128 : b2 + 256].astype(BF16)
        up[384:512] = acc[b2 + 256 : b2 + 384].astype(BF16)
        cross[which, 512:640] = acc[b3 : b3 + 128].astype(BF16)
        small[which] = acc[b3 + 128 : ROWS].astype(BF16)

        @pl.when(even)
        def _():
            rh[which] = up[...]
            rdown[which, 0:512] = low[...]
            rdown[which, 512:640] = cross[which, 512:640]
            rup[which, 0:256] = small[which]

        @pl.when(odd)
        def _():
            rh[which] = low[...]
            rup[which, 0:512] = up[...]
            rup[which, 512:640] = cross[which, 512:640]
            rdown[which, 0:256] = small[which]


def pass_on(role, token):
    token[0] = role[0]
    token[1] = role[1]


def add_down(ref, rows, own):
    add_rows(ref, 0, rows[0:256], 1)
    if own:
        add_rows(ref, 256, rows[256:384], 2)
        add_rows(ref, 512, rows[384:512], 4)
    else:
        add_rows(ref, 512, rows[256:384], 1)
        add_rows(ref, 640, rows[384:448], 2)
        add_rows(ref, 256, rows[448:512], 4)


def add_up(ref, rows, own):
    if own:
        add_rows(ref, 768, rows[0:256], 1)
        add_rows(ref, 512, rows[256:384], 2)
        add_rows(ref, 0, rows[384:512], 4)
    else:
        add_rows(ref, 256, rows[0:256], 1)
        add_rows(ref, 640, rows[256:384], 1)
        add_rows(ref, 0, rows[384:448], 4)
        add_rows(ref, 512, rows[448:512], 2)


def moved(array, pairs):
    return lax.ppermute(array, AXES, pairs)


def shape(*dims, dtype=BF16):
    return jax.ShapeDtypeStruct(dims, dtype)


def vmem(limit):
    return pltpu.CompilerParams(vmem_limit_bytes=limit * 2**20)


SMEM = pl.BlockSpec(memory_space=pltpu.SMEM)


def both(rows):
    return pl.BlockSpec((None, 2, rows, PAIR), lambda j: (j, 0, 0, 0))


def own_rows():
    return pl.BlockSpec((None, 1024, PAIR), lambda j: (j, 0, 0))


def columns(start):
    return pl.BlockSpec((1024, PAIR), lambda j: (0, start + j))


TOKEN = shape(2, dtype=jnp.int32)


def pair_rows(role, keys, values, start, pairs):
    def body(role, k, v, out, token, tmp):
        pass_on(role, token)
        for which, own in ((0, k), (1, v)):
            tmp[...] = own[256:768].astype(F32)
            out[which, 0:256] = own[0:256]
            out[which, 256:512] = own[768:1024]
            out[which, 512:768] = mean_rows(tmp, 0, 256, 2)

    return pl.pallas_call(
        body,
        grid=(pairs,),
        in_specs=[SMEM] + [columns(start)] * 2,
        out_specs=[both(768), SMEM],
        out_shape=[shape(pairs, 2, 768, PAIR), TOKEN],
        scratch_shapes=[pltpu.VMEM((512, PAIR), F32)],
        compiler_params=vmem(LIMIT),
        name="pair_rows",
    )(role, keys, values)


def cross_rows(role, keys, values, partner, start, pairs):
    def body(role, k, v, p, near, up_out, down_out, token, spans, tmp, ours):
        even, wrap = role[0] == 0, role[1]
        odd = jnp.logical_not(even)
        pass_on(role, token)

        for which, own in ((0, k), (1, v)):
            tmp[...] = p[which].astype(F32)
            ours[...] = own[...].astype(F32)
            spans[0:128] = mean_rows(ours, 0, 128, 8)
            spans[128:160] = mean_rows(tmp, 0, 32, 8)
            spans[160:192] = mean_rows(tmp, 512, 32, 4)
            spans[192:224] = mean_rows(tmp, 640, 32, 4)
            spans[224:256] = mean_rows(tmp, 256, 32, 8)

            def theirs_down(out):
                out[which, 0:256] = p[which, 0:256]
                out[which, 256:384] = p[which, 512:640]
                out[which, 384:448] = mean_rows(tmp, 640, 64, 2)
                out[which, 448:512] = mean_rows(tmp, 256, 64, 4)

            def theirs_up(out):
                out[which, 0:256] = p[which, 256:512]
                out[which, 256:384] = p[which, 640:768]
                out[which, 384:448] = mean_rows(tmp, 0, 64, 4)
                out[which, 448:512] = mean_rows(tmp, 512, 64, 2)

            @pl.when(even)
            def _():
                theirs_down(near)
                theirs_up(up_out)
                up_out[which, 512:640] = spans[0:128]
                down_out[which, 0:256] = spans[...]

            @pl.when(odd)
            def _():
                theirs_up(near)
                theirs_down(down_out)
                down_out[which, 512:640] = spans[0:128]
                up_out[which, 0:256] = spans[...]

            @pl.when((wrap == 1) & even)
            def _():
                down_out[which, 0:256] = own[0:256]
                down_out[which, 256:384] = mean_rows(ours, 256, 128, 2)
                down_out[which, 384:512] = mean_rows(ours, 512, 128, 4)
                down_out[which, 512:640] = spans[128:256]

            @pl.when((wrap == 1) & odd)
            def _():
                up_out[which, 0:256] = own[768:1024]
                up_out[which, 256:384] = mean_rows(ours, 512, 128, 2)
                up_out[which, 384:512] = mean_rows(ours, 0, 128, 4)
                up_out[which, 512:640] = spans[128:256]

            @pl.when((wrap == 2) & even)
            def _():
                up_out[which, 0:128] = spans[128:256]
                up_out[which, 128:256] = spans[0:128]

            @pl.when((wrap == 2) & odd)
            def _():
                down_out[which, 0:128] = spans[128:256]
                down_out[which, 128:256] = spans[0:128]

    return pl.pallas_call(
        body,
        grid=(pairs,),
        in_specs=[SMEM, columns(start), columns(start), both(768)],
        out_specs=[both(512), both(640), both(640), SMEM],
        out_shape=[shape(pairs, 2, rows, PAIR) for rows in (512, 640, 640)] + [TOKEN],
        scratch_shapes=[
            pltpu.VMEM((256, PAIR), BF16), pltpu.VMEM((768, PAIR), F32), pltpu.VMEM((1024, PAIR), F32),
        ],
        compiler_params=vmem(LIMIT),
        name="cross_rows",
    )(role, keys, values, partner)


def attend(role, valid, queries, keys, values, grad_out, came, before, start, pairs):

    def side(rows, which):
        return pl.BlockSpec((None, None, rows, PAIR), lambda j: (j, which, 0, 0))

    extra = 0 if before is None else 2

    def body(*refs):
        attend_kernel(*refs[:12], *refs[12 + extra :])

    heights = (512, 640, 640)
    whole = shape(1024, queries.shape[1])
    return pl.pallas_call(
        body,
        grid=(pairs,),
        in_specs=[SMEM, SMEM] + [columns(start)] * 4
        + [side(rows, which) for rows in heights for which in (0, 1)]
        + [pl.BlockSpec(memory_space=pl.ANY)] * extra,
        out_specs=[columns(start)] * 2 + [own_rows()] * 2 + [both(rows) for rows in heights]
        + [SMEM],
        out_shape=[whole, whole]
        + [shape(pairs, 1024, PAIR, dtype=F32)] * 2
        + [shape(pairs, 2, rows, PAIR) for rows in heights]
        + [TOKEN],
        input_output_aliases={12: 0, 13: 1} if extra else {},
        scratch_shapes=[
            pltpu.VMEM((ROWS, PAIR), BF16), pltpu.VMEM((ROWS, PAIR), BF16),
            pltpu.VMEM((PAIR, ROWS), BF16), pltpu.VMEM((2, 80, ROWS), BF16),
        ]
        + [pltpu.VMEM((1920, 512), BF16)] * 2
        + [pltpu.VMEM((512, PAIR), BF16)] * 4
        + [pltpu.VMEM((ROWS, PAIR), F32)] * 2
        + [pltpu.VMEM((8, 512), F32)] * 2
        + [
            pltpu.VMEM((1024, PAIR), F32), pltpu.VMEM((768, PAIR), F32),
            pltpu.VMEM((2, 640, PAIR), BF16), pltpu.VMEM((2, 256, PAIR), BF16),
            pltpu.VMEM((2, 2, 512, PAIR), BF16),
            pltpu.SMEM((1,), jnp.int32), pltpu.SMEM((ROWS // 128,), F32),
        ],
        compiler_params=vmem(LIMIT),
        cost_estimate=pl.CostEstimate(
            flops=pairs * 14 * 10**9, bytes_accessed=pairs * 4 * 10**6, transcendentals=0
        ),
        name="attend_pairs",
    )(
        role, valid, queries, keys, values, grad_out,
        *[part for pair in came for part in (pair, pair)], *(before or ()),
    )


def pair_grads(role, near, above, below, pairs):
    def body(role, near, above, below, out, token, tmp):
        even, wrap = role[0] == 0, role[1]
        odd = jnp.logical_not(even)
        pass_on(role, token)

        def add_span(rows):
            add_rows(tmp, 0, rows[0:32], 8)
            add_rows(tmp, 512, rows[32:64], 4)
            add_rows(tmp, 640, rows[64:96], 4)
            add_rows(tmp, 256, rows[96:128], 8)

        for which in (0, 1):
            tmp[...] = jnp.zeros_like(tmp)

            @pl.when(even)
            def _():
                add_down(tmp, near[which], False)

                @pl.when(wrap != 2)
                def _():
                    add_up(tmp, above[which, 0:512], False)

                @pl.when(wrap == 2)
                def _():
                    add_span(above[which, 0:128])

                @pl.when(wrap == 1)
                def _():
                    add_span(below[which, 512:640])

                @pl.when(wrap != 1)
                def _():
                    add_span(below[which, 128:256])

            @pl.when(odd)
            def _():
                add_up(tmp, near[which], False)

                @pl.when(wrap != 2)
                def _():
                    add_down(tmp, below[which, 0:512], False)

                @pl.when(wrap == 2)
                def _():
                    add_span(below[which, 0:128])

                @pl.when(wrap == 1)
                def _():
                    add_span(above[which, 512:640])

                @pl.when(wrap != 1)
                def _():
                    add_span(above[which, 128:256])

            out[which] = tmp[...].astype(BF16)

    return pl.pallas_call(
        body,
        grid=(pairs,),
        in_specs=[SMEM, both(512), both(640), both(640)],
        out_specs=[both(768), SMEM],
        out_shape=[shape(pairs, 2, 768, PAIR), TOKEN],
        scratch_shapes=[pltpu.VMEM((768, PAIR), F32)],
        compiler_params=vmem(LIMIT),
        name="pair_grads",
    )(role, near, above, below)


def finish(role, own_k, own_v, above, below, partner, before, start, pairs):
    extra = 0 if before is None else 2

    def body(*refs):
        role, gk, gv, above, below, got = refs[:6]
        dk, dv, token, tmp = refs[6 + extra :]
        even, wrap = role[0] == 0, role[1]
        odd = jnp.logical_not(even)
        pass_on(role, token)
        for which, own, out in ((0, gk, dk), (1, gv, dv)):
            tmp[...] = own[...]
            add_rows(tmp, 0, got[which, 0:256], 1)
            add_rows(tmp, 768, got[which, 256:512], 1)
            add_rows(tmp, 256, got[which, 512:768], 2)

            for here, large, small, add in ((even, above, below, add_down), (odd, below, above, add_up)):

                @pl.when(here & (wrap != 2))
                def _():
                    add_rows(tmp, 0, large[which, 512:640], 8)

                @pl.when(here & (wrap == 2))
                def _():
                    add_rows(tmp, 0, large[which, 128:256], 8)

                @pl.when(here & (wrap != 1))
                def _():
                    add_rows(tmp, 0, small[which, 0:128], 8)

                @pl.when(here & (wrap == 1))
                def _():
                    add(tmp, small[which, 0:512], True)

            out[...] = tmp[...].astype(BF16)

    whole = shape(1024, 1024)
    return pl.pallas_call(
        body,
        grid=(pairs,),
        in_specs=[SMEM] + [own_rows()] * 2 + [both(640), both(640), both(768)]
        + [pl.BlockSpec(memory_space=pl.ANY)] * extra,
        out_specs=[columns(start)] * 2 + [SMEM],
        out_shape=[whole, whole, TOKEN],
        input_output_aliases={6: 0, 7: 1} if extra else {},
        scratch_shapes=[pltpu.VMEM((1024, PAIR), F32)],
        compiler_params=vmem(LIMIT),
        name="sum_grads",
    )(role, own_k, own_v, above, below, partner, *(before or ()))


def routes(outer, inner):
    count = outer * inner
    up = {i: i + 2 for i in range(count - 2)}
    for a in range(1, outer - 1, 2):
        last = a * inner + inner - 2
        up[last], up[last + 1] = last + 3, last + 2
    return [(i, i ^ 1) for i in range(count)], sorted(up.items())


def local(queries, keys, values, grad_out):
    a, b = lax.axis_index(AXES[0]), lax.axis_index(AXES[1])
    outer, inner = lax.axis_size(AXES[0]), lax.axis_size(AXES[1])
    index = a * inner + b
    count = outer * inner
    partners, up = routes(outer, inner)
    down = [(j, i) for i, j in up]
    above = (a % 2 == 1) & (a < outer - 1) & (b >= inner - 2)
    below = (a % 2 == 0) & (a > 0) & (b < 2)
    ends = (b == 0) | (b == inner - 1)
    odd = index % 2
    wrap = jnp.where(above | below, jnp.where(ends, 1, 2), 0)
    token = jnp.stack([odd, wrap]).astype(jnp.int32)
    sign = 1 - 2 * odd

    def there(step):
        at = index + step * sign
        return (at >= 0) & (at < count)

    valid = jnp.stack(
        [index > 0, index < count - 1, there(-2), there(2), there(3)]
    ).astype(F32)

    starts = [sum(GROUPS[:i]) for i in range(len(GROUPS))]
    partner, came, grown, near, answers, returned = {}, {}, {}, {}, {}, {}
    mixed = grads = None
    for step, i in ORDER:
        start, pairs = starts[i], GROUPS[i]
        if step == "pair":
            rows, token = pair_rows(token, keys, values, start, pairs)
            partner[i] = moved(rows, partners)
        elif step == "cross":
            side, upward, downward, token = cross_rows(
                token, keys, values, partner[i], start, pairs
            )
            came[i] = (side, moved(upward, up), moved(downward, down))
        elif step == "attend":
            *mixed, gk, gv, near[i], upward, downward, token = attend(
                token, valid, queries, keys, values, grad_out, came[i], mixed, start, pairs
            )
            grown[i] = (gk, gv)
            answers[i] = (moved(downward, down), moved(upward, up))
        elif step == "back":
            rows, token = pair_grads(token, near[i], *answers[i], pairs)
            returned[i] = moved(rows, partners)
        else:
            *grads, token = finish(token, *grown[i], *answers[i], returned[i], grads, start, pairs)
    return (*mixed, *grads)


def solution(mesh):
    placed = P(AXES, None)
    return jax.shard_map(
        local,
        mesh=mesh,
        in_specs=(placed,) * 4,
        out_specs=(placed,) * 4,
        check_vma=False,
    )
```

```python
import math

import jax
import jax.numpy as jnp
from jax import lax
from jax.experimental import pallas as pl
from jax.experimental.pallas import tpu as pltpu
from jax.sharding import PartitionSpec as P

HEAD_DIM = 64
BLOCK = 256
HALF = 128
PAIR = 128
AXES = ("seqa", "seqb")
GROUPS = (1, 3, 3, 1)
ORDER = (
    ("pair", 0), ("cross", 0), ("pair", 1),
    ("attend", 0), ("cross", 1), ("pair", 2), ("cross", 2), ("pair", 3),
    ("attend", 1), ("cross", 3), ("back", 0),
    ("attend", 2), ("back", 1),
    ("attend", 3), ("back", 2), ("sum", 0), ("back", 3), ("sum", 1), ("sum", 2), ("sum", 3),
)
LIMIT = 60
LOG2E = math.log2(math.e)
BF16 = jnp.bfloat16
F32 = jnp.float32
NT = (((1,), (1,)), ((), ()))
NN = (((1,), (0,)), ((), ()))

BASE = (0, 1536, 2560, 3072)
ROWS = 3456

PIECES = ((768, 0), (384, 768), (384, 1152), (384, 1536))


def piece_starts(b):
    half = b // 2
    first = BASE[1] + half * 512 + (1 - (b - 2 * half)) * 128
    rows = (b * 256, first, BASE[2] + half * 128, BASE[3])
    return [r if isinstance(r, int) else pl.multiple_of(r, 128) for r in rows]


def dot(a, b, dims=NN):
    return lax.dot_general(a, b, dims, preferred_element_type=F32)


def mean_rows(ref, start, count, stride):
    total = ref[pl.ds(start, count, stride=stride), :]
    for i in range(1, stride):
        total = total + ref[pl.ds(start + i, count, stride=stride), :]
    return (total * (1.0 / stride)).astype(BF16)


def add_rows(ref, start, rows, stride):
    if stride == 1:
        at = slice(start, start + rows.shape[0])
        ref[at] = ref[at] + rows.astype(F32)
    else:
        spread_rows(ref, start, rows.astype(F32), stride)


def spread_rows(ref, start, rows, stride):
    for i in range(stride):
        at = pl.ds(start + i, rows.shape[0], stride=stride)
        ref[at, :] = ref[at, :] + rows


def attend_kernel(
    role, valid, q, k, v, do, hk, hv, bk, bv, ak, av,
    o, dq, gk, gv, rh, rup, rdown, token,
    kext, vext, kt, vt, e, x, qz, doz, qs, dos, acck, accv, inn, rls, ftmp, gtmp,
    cross, small, side, flag, oks,
):
    lane = lax.broadcasted_iota(jnp.int32, (256, PAIR), 1)
    first = lane < HEAD_DIM
    even = role[0] == 0
    odd = jnp.logical_not(even)
    pass_on(role, token)

    for which, (h, b, a) in enumerate(((hk, bk, ak), (hv, bv, av))):

        @pl.when(even)
        def _():
            cross[which] = b[...]
            small[which] = a[0:256]
            side[0, which] = b[0:512]
            side[1, which] = h[...]

        @pl.when(odd)
        def _():
            cross[which] = a[...]
            small[which] = b[0:256]
            side[0, which] = h[...]
            side[1, which] = a[0:512]

    for which, own, ext in ((0, k, kext), (1, v, vext)):
        low, up = side.at[0, which], side.at[1, which]
        ext[0:256] = low[0:256]
        ext[256:1280] = own[...]
        ext[1280:1536] = up[0:256]
        ftmp[...] = own[...].astype(F32)
        spans = mean_rows(ftmp, 0, 512, 2)
        b1 = BASE[1]
        ext[b1 + 256 : b1 + 384] = spans[384:512]
        ext[b1 + 384 : b1 + 512] = spans[256:384]
        ext[b1 + 512 : b1 + 640] = spans[128:256]
        ext[b1 + 640 : b1 + 768] = spans[0:128]
        ext[b1 + 128 : b1 + 256] = low[256:384]
        ext[b1 + 768 : b1 + 896] = up[256:384]
        b2 = BASE[2]
        ftmp[0:384] = low[0:384].astype(F32)
        ext[b1 : b1 + 128] = mean_rows(ftmp, 0, 128, 2)
        ext[b2 + 384 : b2 + 448] = mean_rows(ftmp, 256, 64, 2)
        ext[b2 + 448 : b2 + 512] = mean_rows(ftmp, 0, 64, 4)
        ftmp[0:384] = up[0:384].astype(F32)
        ext[b1 + 896 : b1 + 1024] = mean_rows(ftmp, 0, 128, 2)
        ext[b2 : b2 + 64] = mean_rows(ftmp, 0, 64, 4)
        ext[b2 + 64 : b2 + 128] = mean_rows(ftmp, 256, 64, 2)
        ext[b2 + 128 : b2 + 256] = low[384:512]
        ext[b2 + 256 : b2 + 384] = up[384:512]
        ext[BASE[3] : BASE[3] + 128] = cross[which, 512:640]
        ext[BASE[3] + 128 : ROWS] = small[which]

    low_ok, up_ok = valid[0], valid[1]
    for level, row, rows, ok in (
        (0, 0, 256, low_ok), (0, 256, 1024, 1.0), (0, 1280, 256, up_ok),
        (1, 0, 256, low_ok), (1, 256, 512, 1.0), (1, 768, 256, up_ok),
        (2, 0, 128, up_ok), (2, 128, 128, low_ok), (2, 256, 128, up_ok), (2, 384, 128, low_ok),
        (3, 0, 128, valid[2]), (3, 128, 128, valid[3]), (3, 256, 128, valid[4]),
    ):
        at = slice(BASE[level] + row, BASE[level] + row + rows)
        for i in range(at.start // 128, at.stop // 128):
            oks[i] = ok
        scale = float(2**level)
        kt[:, at] = (kext[at] * scale).astype(BF16).T
        vals = (vext[at] * scale).astype(BF16).T
        top = lax.broadcasted_iota(jnp.int32, (16, rows), 0) == 0
        ones = jnp.where(top, ok * scale, 0.0).astype(BF16)
        for h in range(2):
            vt[h, 0:64, at] = vals[h * 64 : h * 64 + 64]
            vt[h, 64:80, at] = ones

    acck[...] = jnp.zeros_like(acck)
    accv[...] = jnp.zeros_like(accv)

    def block_step(b, carry):
        at = pl.ds(pl.multiple_of(b * 256, 256), 256)
        starts = piece_starts(b)
        spots = [(pl.ds(r, n), slice(to, to + n)) for r, (n, to) in zip(starts, PIECES)]
        query, grad = q[at].astype(F32), do[at].astype(F32)
        heads = (slice(0, 256), slice(256, 512))
        for h in range(2):
            mine = first if h == 0 else ~first
            qz[heads[h]] = jnp.where(mine, query * 0.125, 0.0).astype(BF16)
            doz[heads[h]] = jnp.where(mine, grad, 0.0).astype(BF16)

        for rows, to in spots:
            for h in heads:
                s = dot(kext[rows], qz[h], NT)
                e[to, h] = jnp.exp2(s * LOG2E).astype(BF16)

        def forward():
            outs, recips = [], []
            least, most = None, None
            for h in range(2):
                acc = jnp.zeros((80, 256), F32)
                for rows, to in spots:
                    acc = acc + dot(vt[h, :, rows], e[to, heads[h]])
                total = acc[64:65]
                least = total if least is None else jnp.minimum(least, total)
                most = total if most is None else jnp.maximum(most, total)
                recip = 1.0 / total
                outs.append(acc[0:64] * recip)
                recips.append(recip)
            fine = (jnp.min(least) > 2.0**-60) & (jnp.max(most) < 2.0**60)
            flag[0] = jnp.where(fine, 0, 1)
            return outs, recips

        def settle(outs, recips):
            mixed = jnp.concatenate(outs, 0)
            o[at] = mixed.T.astype(BF16)
            prod = mixed.astype(BF16).astype(F32) * grad.T
            wide = jnp.concatenate([jnp.broadcast_to(r, (64, 256)) for r in recips], 0).T
            for h in range(2):
                inn[0:1, heads[h]] = jnp.sum(prod[h * 64 : h * 64 + 64], axis=0, keepdims=True)
                rls[0:1, heads[h]] = recips[h]
                mine = first if h == 0 else ~first
                dos[heads[h]] = jnp.where(mine, grad * wide, 0.0).astype(BF16)
                qs[heads[h]] = jnp.where(mine, query * (wide * 0.125), 0.0).astype(BF16)

        settle(*forward())

        @pl.when(flag[0] == 1)
        def _():
            for h in heads:

                def scores(row):
                    row = pl.multiple_of(row, 128)
                    s = dot(kext[pl.ds(row, 128)], qz[h], NT) * LOG2E
                    return jnp.where(oks[row // 128] > 0.5, s, -jnp.inf)

                highest = jnp.full((1, 256), -jnp.inf, F32)
                for r, (n, to) in zip(starts, PIECES):
                    highest = lax.fori_loop(
                        0,
                        n // 128,
                        lambda t, top: jnp.maximum(
                            top, jnp.max(scores(r + t * 128), axis=0, keepdims=True)
                        ),
                        highest,
                    )
                for r, (n, to) in zip(starts, PIECES):

                    def again(t, carry):
                        put = pl.ds(pl.multiple_of(to + t * 128, 128), 128)
                        e[put, h] = jnp.exp2(scores(r + t * 128) - highest).astype(BF16)
                        return carry

                    lax.fori_loop(0, n // 128, again, 0)
            settle(*forward())

        for rows, to in spots:
            for h in heads:
                dp = dot(vext[rows], doz[h], NT) - inn[0:1, h]
                x[to, h] = e[to, h] * dp.astype(BF16)

        outs = []
        for h in range(2):
            acc = jnp.zeros((64, 256), F32)
            for rows, to in spots:
                acc = acc + dot(kt[h * 64 : h * 64 + 64, rows], x[to, heads[h]])
            outs.append(acc * (rls[0:1, heads[h]] * 0.125))
        dq[at] = jnp.concatenate(outs, 0).T.astype(BF16)

        for rows, to in spots:
            acck[rows] = acck[rows] + dot(x[to], qs[...])
            accv[rows] = accv[rows] + dot(e[to], dos[...])
        return carry

    lax.fori_loop(0, 4, block_step, 0)

    b1, b2, b3 = BASE[1:]
    for which, acc, own in ((0, acck, gk), (1, accv, gv)):
        low, up = side.at[0, which], side.at[1, which]
        own[...] = acc[256:1280]
        for i, row in enumerate((640, 512, 384, 256)):
            spread_rows(own, i * 256, acc[b1 + row : b1 + row + 128], 2)
        gtmp[0:256] = acc[0:256]
        spread_rows(gtmp, 0, acc[b1 : b1 + 128], 2)
        spread_rows(gtmp, 0, acc[b2 + 448 : b2 + 512], 4)
        gtmp[256:384] = acc[b1 + 128 : b1 + 256]
        spread_rows(gtmp, 256, acc[b2 + 384 : b2 + 448], 2)
        gtmp[384:640] = acc[1280:1536]
        spread_rows(gtmp, 384, acc[b1 + 896 : b1 + 1024], 2)
        spread_rows(gtmp, 384, acc[b2 : b2 + 64], 4)
        gtmp[640:768] = acc[b1 + 768 : b1 + 896]
        spread_rows(gtmp, 640, acc[b2 + 64 : b2 + 128], 2)
        low[0:384] = gtmp[0:384].astype(BF16)
        up[0:384] = gtmp[384:768].astype(BF16)
        low[384:512] = acc[b2 + 128 : b2 + 256].astype(BF16)
        up[384:512] = acc[b2 + 256 : b2 + 384].astype(BF16)
        cross[which, 512:640] = acc[b3 : b3 + 128].astype(BF16)
        small[which] = acc[b3 + 128 : ROWS].astype(BF16)

        @pl.when(even)
        def _():
            rh[which] = up[...]
            rdown[which, 0:512] = low[...]
            rdown[which, 512:640] = cross[which, 512:640]
            rup[which, 0:256] = small[which]

        @pl.when(odd)
        def _():
            rh[which] = low[...]
            rup[which, 0:512] = up[...]
            rup[which, 512:640] = cross[which, 512:640]
            rdown[which, 0:256] = small[which]


def pass_on(role, token):
    token[0] = role[0]
    token[1] = role[1]


def add_down(ref, rows, own):
    add_rows(ref, 0, rows[0:256], 1)
    if own:
        add_rows(ref, 256, rows[256:384], 2)
        add_rows(ref, 512, rows[384:512], 4)
    else:
        add_rows(ref, 512, rows[256:384], 1)
        add_rows(ref, 640, rows[384:448], 2)
        add_rows(ref, 256, rows[448:512], 4)


def add_up(ref, rows, own):
    if own:
        add_rows(ref, 768, rows[0:256], 1)
        add_rows(ref, 512, rows[256:384], 2)
        add_rows(ref, 0, rows[384:512], 4)
    else:
        add_rows(ref, 256, rows[0:256], 1)
        add_rows(ref, 640, rows[256:384], 1)
        add_rows(ref, 0, rows[384:448], 4)
        add_rows(ref, 512, rows[448:512], 2)


def moved(array, pairs):
    return lax.ppermute(array, AXES, pairs)


def shape(*dims, dtype=BF16):
    return jax.ShapeDtypeStruct(dims, dtype)


def vmem(limit):
    return pltpu.CompilerParams(vmem_limit_bytes=limit * 2**20)


SMEM = pl.BlockSpec(memory_space=pltpu.SMEM)


def both(rows):
    return pl.BlockSpec((None, 2, rows, PAIR), lambda j: (j, 0, 0, 0))


def own_rows():
    return pl.BlockSpec((None, 1024, PAIR), lambda j: (j, 0, 0))


def columns(start):
    return pl.BlockSpec((1024, PAIR), lambda j: (0, start + j))


TOKEN = shape(2, dtype=jnp.int32)


def pair_rows(role, keys, values, start, pairs):
    def body(role, k, v, out, token, tmp):
        pass_on(role, token)
        for which, own in ((0, k), (1, v)):
            tmp[...] = own[256:768].astype(F32)
            out[which, 0:256] = own[0:256]
            out[which, 256:512] = own[768:1024]
            out[which, 512:768] = mean_rows(tmp, 0, 256, 2)

    return pl.pallas_call(
        body,
        grid=(pairs,),
        in_specs=[SMEM] + [columns(start)] * 2,
        out_specs=[both(768), SMEM],
        out_shape=[shape(pairs, 2, 768, PAIR), TOKEN],
        scratch_shapes=[pltpu.VMEM((512, PAIR), F32)],
        compiler_params=vmem(LIMIT),
        name="pair_rows",
    )(role, keys, values)


def cross_rows(role, keys, values, partner, start, pairs):
    def body(role, k, v, p, near, up_out, down_out, token, spans, tmp, ours):
        even, wrap = role[0] == 0, role[1]
        odd = jnp.logical_not(even)
        pass_on(role, token)

        for which, own in ((0, k), (1, v)):
            tmp[...] = p[which].astype(F32)
            ours[...] = own[...].astype(F32)
            spans[0:128] = mean_rows(ours, 0, 128, 8)
            spans[128:160] = mean_rows(tmp, 0, 32, 8)
            spans[160:192] = mean_rows(tmp, 512, 32, 4)
            spans[192:224] = mean_rows(tmp, 640, 32, 4)
            spans[224:256] = mean_rows(tmp, 256, 32, 8)

            def theirs_down(out):
                out[which, 0:256] = p[which, 0:256]
                out[which, 256:384] = p[which, 512:640]
                out[which, 384:448] = mean_rows(tmp, 640, 64, 2)
                out[which, 448:512] = mean_rows(tmp, 256, 64, 4)

            def theirs_up(out):
                out[which, 0:256] = p[which, 256:512]
                out[which, 256:384] = p[which, 640:768]
                out[which, 384:448] = mean_rows(tmp, 0, 64, 4)
                out[which, 448:512] = mean_rows(tmp, 512, 64, 2)

            @pl.when(even)
            def _():
                theirs_down(near)
                theirs_up(up_out)
                up_out[which, 512:640] = spans[0:128]
                down_out[which, 0:256] = spans[...]

            @pl.when(odd)
            def _():
                theirs_up(near)
                theirs_down(down_out)
                down_out[which, 512:640] = spans[0:128]
                up_out[which, 0:256] = spans[...]

            @pl.when((wrap == 1) & even)
            def _():
                down_out[which, 0:256] = own[0:256]
                down_out[which, 256:384] = mean_rows(ours, 256, 128, 2)
                down_out[which, 384:512] = mean_rows(ours, 512, 128, 4)
                down_out[which, 512:640] = spans[128:256]

            @pl.when((wrap == 1) & odd)
            def _():
                up_out[which, 0:256] = own[768:1024]
                up_out[which, 256:384] = mean_rows(ours, 512, 128, 2)
                up_out[which, 384:512] = mean_rows(ours, 0, 128, 4)
                up_out[which, 512:640] = spans[128:256]

            @pl.when((wrap == 2) & even)
            def _():
                up_out[which, 0:128] = spans[128:256]
                up_out[which, 128:256] = spans[0:128]

            @pl.when((wrap == 2) & odd)
            def _():
                down_out[which, 0:128] = spans[128:256]
                down_out[which, 128:256] = spans[0:128]

    return pl.pallas_call(
        body,
        grid=(pairs,),
        in_specs=[SMEM, columns(start), columns(start), both(768)],
        out_specs=[both(512), both(640), both(640), SMEM],
        out_shape=[shape(pairs, 2, rows, PAIR) for rows in (512, 640, 640)] + [TOKEN],
        scratch_shapes=[
            pltpu.VMEM((256, PAIR), BF16), pltpu.VMEM((768, PAIR), F32), pltpu.VMEM((1024, PAIR), F32),
        ],
        compiler_params=vmem(LIMIT),
        name="cross_rows",
    )(role, keys, values, partner)


def attend(role, valid, queries, keys, values, grad_out, came, before, start, pairs):

    def side(rows, which):
        return pl.BlockSpec((None, None, rows, PAIR), lambda j: (j, which, 0, 0))

    extra = 0 if before is None else 2

    def body(*refs):
        attend_kernel(*refs[:12], *refs[12 + extra :])

    heights = (512, 640, 640)
    whole = shape(1024, queries.shape[1])
    return pl.pallas_call(
        body,
        grid=(pairs,),
        in_specs=[SMEM, SMEM] + [columns(start)] * 4
        + [side(rows, which) for rows in heights for which in (0, 1)]
        + [pl.BlockSpec(memory_space=pl.ANY)] * extra,
        out_specs=[columns(start)] * 2 + [own_rows()] * 2 + [both(rows) for rows in heights]
        + [SMEM],
        out_shape=[whole, whole]
        + [shape(pairs, 1024, PAIR, dtype=F32)] * 2
        + [shape(pairs, 2, rows, PAIR) for rows in heights]
        + [TOKEN],
        input_output_aliases={12: 0, 13: 1} if extra else {},
        scratch_shapes=[
            pltpu.VMEM((ROWS, PAIR), BF16), pltpu.VMEM((ROWS, PAIR), BF16),
            pltpu.VMEM((PAIR, ROWS), BF16), pltpu.VMEM((2, 80, ROWS), BF16),
        ]
        + [pltpu.VMEM((1920, 512), BF16)] * 2
        + [pltpu.VMEM((512, PAIR), BF16)] * 4
        + [pltpu.VMEM((ROWS, PAIR), F32)] * 2
        + [pltpu.VMEM((8, 512), F32)] * 2
        + [
            pltpu.VMEM((1024, PAIR), F32), pltpu.VMEM((768, PAIR), F32),
            pltpu.VMEM((2, 640, PAIR), BF16), pltpu.VMEM((2, 256, PAIR), BF16),
            pltpu.VMEM((2, 2, 512, PAIR), BF16),
            pltpu.SMEM((1,), jnp.int32), pltpu.SMEM((ROWS // 128,), F32),
        ],
        compiler_params=vmem(LIMIT),
        cost_estimate=pl.CostEstimate(
            flops=pairs * 14 * 10**9, bytes_accessed=pairs * 4 * 10**6, transcendentals=0
        ),
        name="attend_pairs",
    )(
        role, valid, queries, keys, values, grad_out,
        *[part for pair in came for part in (pair, pair)], *(before or ()),
    )


def pair_grads(role, near, above, below, pairs):
    def body(role, near, above, below, out, token, tmp):
        even, wrap = role[0] == 0, role[1]
        odd = jnp.logical_not(even)
        pass_on(role, token)

        def add_span(rows):
            add_rows(tmp, 0, rows[0:32], 8)
            add_rows(tmp, 512, rows[32:64], 4)
            add_rows(tmp, 640, rows[64:96], 4)
            add_rows(tmp, 256, rows[96:128], 8)

        for which in (0, 1):
            tmp[...] = jnp.zeros_like(tmp)

            @pl.when(even)
            def _():
                add_down(tmp, near[which], False)

                @pl.when(wrap != 2)
                def _():
                    add_up(tmp, above[which, 0:512], False)

                @pl.when(wrap == 2)
                def _():
                    add_span(above[which, 0:128])

                @pl.when(wrap == 1)
                def _():
                    add_span(below[which, 512:640])

                @pl.when(wrap != 1)
                def _():
                    add_span(below[which, 128:256])

            @pl.when(odd)
            def _():
                add_up(tmp, near[which], False)

                @pl.when(wrap != 2)
                def _():
                    add_down(tmp, below[which, 0:512], False)

                @pl.when(wrap == 2)
                def _():
                    add_span(below[which, 0:128])

                @pl.when(wrap == 1)
                def _():
                    add_span(above[which, 512:640])

                @pl.when(wrap != 1)
                def _():
                    add_span(above[which, 128:256])

            out[which] = tmp[...].astype(BF16)

    return pl.pallas_call(
        body,
        grid=(pairs,),
        in_specs=[SMEM, both(512), both(640), both(640)],
        out_specs=[both(768), SMEM],
        out_shape=[shape(pairs, 2, 768, PAIR), TOKEN],
        scratch_shapes=[pltpu.VMEM((768, PAIR), F32)],
        compiler_params=vmem(LIMIT),
        name="pair_grads",
    )(role, near, above, below)


def finish(role, own_k, own_v, above, below, partner, before, start, pairs):
    extra = 0 if before is None else 2

    def body(*refs):
        role, gk, gv, above, below, got = refs[:6]
        dk, dv, token, tmp = refs[6 + extra :]
        even, wrap = role[0] == 0, role[1]
        odd = jnp.logical_not(even)
        pass_on(role, token)
        for which, own, out in ((0, gk, dk), (1, gv, dv)):
            tmp[...] = own[...]
            add_rows(tmp, 0, got[which, 0:256], 1)
            add_rows(tmp, 768, got[which, 256:512], 1)
            add_rows(tmp, 256, got[which, 512:768], 2)

            for here, large, small, add in ((even, above, below, add_down), (odd, below, above, add_up)):

                @pl.when(here & (wrap != 2))
                def _():
                    add_rows(tmp, 0, large[which, 512:640], 8)

                @pl.when(here & (wrap == 2))
                def _():
                    add_rows(tmp, 0, large[which, 128:256], 8)

                @pl.when(here & (wrap != 1))
                def _():
                    add_rows(tmp, 0, small[which, 0:128], 8)

                @pl.when(here & (wrap == 1))
                def _():
                    add(tmp, small[which, 0:512], True)

            out[...] = tmp[...].astype(BF16)

    whole = shape(1024, 1024)
    return pl.pallas_call(
        body,
        grid=(pairs,),
        in_specs=[SMEM] + [own_rows()] * 2 + [both(640), both(640), both(768)]
        + [pl.BlockSpec(memory_space=pl.ANY)] * extra,
        out_specs=[columns(start)] * 2 + [SMEM],
        out_shape=[whole, whole, TOKEN],
        input_output_aliases={6: 0, 7: 1} if extra else {},
        scratch_shapes=[pltpu.VMEM((1024, PAIR), F32)],
        compiler_params=vmem(LIMIT),
        name="sum_grads",
    )(role, own_k, own_v, above, below, partner, *(before or ()))


def routes(outer, inner):
    count = outer * inner
    up = {i: i + 2 for i in range(count - 2)}
    for a in range(1, outer - 1, 2):
        last = a * inner + inner - 2
        up[last], up[last + 1] = last + 3, last + 2
    return [(i, i ^ 1) for i in range(count)], sorted(up.items())


def local(queries, keys, values, grad_out):
    a, b = lax.axis_index(AXES[0]), lax.axis_index(AXES[1])
    outer, inner = lax.axis_size(AXES[0]), lax.axis_size(AXES[1])
    index = a * inner + b
    count = outer * inner
    partners, up = routes(outer, inner)
    down = [(j, i) for i, j in up]
    above = (a % 2 == 1) & (a < outer - 1) & (b >= inner - 2)
    below = (a % 2 == 0) & (a > 0) & (b < 2)
    ends = (b == 0) | (b == inner - 1)
    odd = index % 2
    wrap = jnp.where(above | below, jnp.where(ends, 1, 2), 0)
    token = jnp.stack([odd, wrap]).astype(jnp.int32)
    sign = 1 - 2 * odd

    def there(step):
        at = index + step * sign
        return (at >= 0) & (at < count)

    valid = jnp.stack(
        [index > 0, index < count - 1, there(-2), there(2), there(3)]
    ).astype(F32)

    starts = [sum(GROUPS[:i]) for i in range(len(GROUPS))]
    partner, came, grown, near, answers, returned = {}, {}, {}, {}, {}, {}
    mixed = grads = None
    for step, i in ORDER:
        start, pairs = starts[i], GROUPS[i]
        if step == "pair":
            rows, token = pair_rows(token, keys, values, start, pairs)
            partner[i] = moved(rows, partners)
        elif step == "cross":
            side, upward, downward, token = cross_rows(
                token, keys, values, partner[i], start, pairs
            )
            came[i] = (side, moved(upward, up), moved(downward, down))
        elif step == "attend":
            *mixed, gk, gv, near[i], upward, downward, token = attend(
                token, valid, queries, keys, values, grad_out, came[i], mixed, start, pairs
            )
            grown[i] = (gk, gv)
            answers[i] = (moved(downward, down), moved(upward, up))
        elif step == "back":
            rows, token = pair_grads(token, near[i], *answers[i], pairs)
            returned[i] = moved(rows, partners)
        else:
            *grads, token = finish(token, *grown[i], *answers[i], returned[i], grads, start, pairs)
    return (*mixed, *grads)


def solution(mesh):
    placed = P(AXES, None)
    return jax.shard_map(
        local,
        mesh=mesh,
        in_specs=(placed,) * 4,
        out_specs=(placed,) * 4,
        check_vma=False,
    )
```

```python
import math

import jax
import jax.numpy as jnp
from jax import lax
from jax.experimental import pallas as pl
from jax.experimental.pallas import tpu as pltpu
from jax.sharding import PartitionSpec as P

HEAD_DIM = 64
BLOCK = 256
HALF = 128
PAIR = 128
AXES = ("seqa", "seqb")
GROUPS = (2, 3, 2, 1)
ORDER = (
    ("pair", 0), ("cross", 0), ("pair", 1),
    ("attend", 0), ("cross", 1), ("pair", 2), ("cross", 2), ("pair", 3),
    ("attend", 1), ("cross", 3), ("back", 0),
    ("attend", 2), ("back", 1),
    ("attend", 3), ("back", 2), ("sum", 0), ("back", 3), ("sum", 1), ("sum", 2), ("sum", 3),
)
LIMIT = 60
LOG2E = math.log2(math.e)
BF16 = jnp.bfloat16
F32 = jnp.float32
NT = (((1,), (1,)), ((), ()))
NN = (((1,), (0,)), ((), ()))

BASE = (0, 1536, 2560, 3072)
ROWS = 3456

PIECES = ((768, 0), (384, 768), (384, 1152), (384, 1536))


def piece_starts(b):
    half = b // 2
    first = BASE[1] + half * 512 + (1 - (b - 2 * half)) * 128
    rows = (b * 256, first, BASE[2] + half * 128, BASE[3])
    return [r if isinstance(r, int) else pl.multiple_of(r, 128) for r in rows]


def dot(a, b, dims=NN):
    return lax.dot_general(a, b, dims, preferred_element_type=F32)


def mean_rows(ref, start, count, stride):
    total = ref[pl.ds(start, count, stride=stride), :]
    for i in range(1, stride):
        total = total + ref[pl.ds(start + i, count, stride=stride), :]
    return (total * (1.0 / stride)).astype(BF16)


def add_rows(ref, start, rows, stride):
    if stride == 1:
        at = slice(start, start + rows.shape[0])
        ref[at] = ref[at] + rows.astype(F32)
    else:
        spread_rows(ref, start, rows.astype(F32), stride)


def spread_rows(ref, start, rows, stride):
    for i in range(stride):
        at = pl.ds(start + i, rows.shape[0], stride=stride)
        ref[at, :] = ref[at, :] + rows


def attend_kernel(
    role, valid, q, k, v, do, hk, hv, bk, bv, ak, av,
    o, dq, gk, gv, rh, rup, rdown, token,
    kext, vext, kt, vt, e, x, qz, doz, qs, dos, acck, accv, inn, rls, ftmp, gtmp,
    cross, small, side, flag, oks,
):
    lane = lax.broadcasted_iota(jnp.int32, (256, PAIR), 1)
    first = lane < HEAD_DIM
    even = role[0] == 0
    odd = jnp.logical_not(even)
    pass_on(role, token)

    for which, (h, b, a) in enumerate(((hk, bk, ak), (hv, bv, av))):

        @pl.when(even)
        def _():
            cross[which] = b[...]
            small[which] = a[0:256]
            side[0, which] = b[0:512]
            side[1, which] = h[...]

        @pl.when(odd)
        def _():
            cross[which] = a[...]
            small[which] = b[0:256]
            side[0, which] = h[...]
            side[1, which] = a[0:512]

    for which, own, ext in ((0, k, kext), (1, v, vext)):
        low, up = side.at[0, which], side.at[1, which]
        ext[0:256] = low[0:256]
        ext[256:1280] = own[...]
        ext[1280:1536] = up[0:256]
        ftmp[...] = own[...].astype(F32)
        spans = mean_rows(ftmp, 0, 512, 2)
        b1 = BASE[1]
        ext[b1 + 256 : b1 + 384] = spans[384:512]
        ext[b1 + 384 : b1 + 512] = spans[256:384]
        ext[b1 + 512 : b1 + 640] = spans[128:256]
        ext[b1 + 640 : b1 + 768] = spans[0:128]
        ext[b1 + 128 : b1 + 256] = low[256:384]
        ext[b1 + 768 : b1 + 896] = up[256:384]
        b2 = BASE[2]
        ftmp[0:384] = low[0:384].astype(F32)
        ext[b1 : b1 + 128] = mean_rows(ftmp, 0, 128, 2)
        ext[b2 + 384 : b2 + 448] = mean_rows(ftmp, 256, 64, 2)
        ext[b2 + 448 : b2 + 512] = mean_rows(ftmp, 0, 64, 4)
        ftmp[0:384] = up[0:384].astype(F32)
        ext[b1 + 896 : b1 + 1024] = mean_rows(ftmp, 0, 128, 2)
        ext[b2 : b2 + 64] = mean_rows(ftmp, 0, 64, 4)
        ext[b2 + 64 : b2 + 128] = mean_rows(ftmp, 256, 64, 2)
        ext[b2 + 128 : b2 + 256] = low[384:512]
        ext[b2 + 256 : b2 + 384] = up[384:512]
        ext[BASE[3] : BASE[3] + 128] = cross[which, 512:640]
        ext[BASE[3] + 128 : ROWS] = small[which]

    low_ok, up_ok = valid[0], valid[1]
    for level, row, rows, ok in (
        (0, 0, 256, low_ok), (0, 256, 1024, 1.0), (0, 1280, 256, up_ok),
        (1, 0, 256, low_ok), (1, 256, 512, 1.0), (1, 768, 256, up_ok),
        (2, 0, 128, up_ok), (2, 128, 128, low_ok), (2, 256, 128, up_ok), (2, 384, 128, low_ok),
        (3, 0, 128, valid[2]), (3, 128, 128, valid[3]), (3, 256, 128, valid[4]),
    ):
        at = slice(BASE[level] + row, BASE[level] + row + rows)
        for i in range(at.start // 128, at.stop // 128):
            oks[i] = ok
        scale = float(2**level)
        kt[:, at] = (kext[at] * scale).astype(BF16).T
        vals = (vext[at] * scale).astype(BF16).T
        top = lax.broadcasted_iota(jnp.int32, (16, rows), 0) == 0
        ones = jnp.where(top, ok * scale, 0.0).astype(BF16)
        for h in range(2):
            vt[h, 0:64, at] = vals[h * 64 : h * 64 + 64]
            vt[h, 64:80, at] = ones

    acck[...] = jnp.zeros_like(acck)
    accv[...] = jnp.zeros_like(accv)

    def block_step(b, carry):
        at = pl.ds(pl.multiple_of(b * 256, 256), 256)
        starts = piece_starts(b)
        spots = [(pl.ds(r, n), slice(to, to + n)) for r, (n, to) in zip(starts, PIECES)]
        query, grad = q[at].astype(F32), do[at].astype(F32)
        heads = (slice(0, 256), slice(256, 512))
        for h in range(2):
            mine = first if h == 0 else ~first
            qz[heads[h]] = jnp.where(mine, query * 0.125, 0.0).astype(BF16)
            doz[heads[h]] = jnp.where(mine, grad, 0.0).astype(BF16)

        for rows, to in spots:
            for h in heads:
                s = dot(kext[rows], qz[h], NT)
                e[to, h] = jnp.exp2(s * LOG2E).astype(BF16)

        def forward():
            outs, recips = [], []
            least, most = None, None
            for h in range(2):
                acc = jnp.zeros((80, 256), F32)
                for rows, to in spots:
                    acc = acc + dot(vt[h, :, rows], e[to, heads[h]])
                total = acc[64:65]
                least = total if least is None else jnp.minimum(least, total)
                most = total if most is None else jnp.maximum(most, total)
                recip = 1.0 / total
                outs.append(acc[0:64] * recip)
                recips.append(recip)
            fine = (jnp.min(least) > 2.0**-60) & (jnp.max(most) < 2.0**60)
            flag[0] = jnp.where(fine, 0, 1)
            return outs, recips

        def settle(outs, recips):
            mixed = jnp.concatenate(outs, 0)
            o[at] = mixed.T.astype(BF16)
            prod = mixed.astype(BF16).astype(F32) * grad.T
            wide = jnp.concatenate([jnp.broadcast_to(r, (64, 256)) for r in recips], 0).T
            for h in range(2):
                inn[0:1, heads[h]] = jnp.sum(prod[h * 64 : h * 64 + 64], axis=0, keepdims=True)
                rls[0:1, heads[h]] = recips[h]
                mine = first if h == 0 else ~first
                dos[heads[h]] = jnp.where(mine, grad * wide, 0.0).astype(BF16)
                qs[heads[h]] = jnp.where(mine, query * (wide * 0.125), 0.0).astype(BF16)

        settle(*forward())

        @pl.when(flag[0] == 1)
        def _():
            for h in heads:

                def scores(row):
                    row = pl.multiple_of(row, 128)
                    s = dot(kext[pl.ds(row, 128)], qz[h], NT) * LOG2E
                    return jnp.where(oks[row // 128] > 0.5, s, -jnp.inf)

                highest = jnp.full((1, 256), -jnp.inf, F32)
                for r, (n, to) in zip(starts, PIECES):
                    highest = lax.fori_loop(
                        0,
                        n // 128,
                        lambda t, top: jnp.maximum(
                            top, jnp.max(scores(r + t * 128), axis=0, keepdims=True)
                        ),
                        highest,
                    )
                for r, (n, to) in zip(starts, PIECES):

                    def again(t, carry):
                        put = pl.ds(pl.multiple_of(to + t * 128, 128), 128)
                        e[put, h] = jnp.exp2(scores(r + t * 128) - highest).astype(BF16)
                        return carry

                    lax.fori_loop(0, n // 128, again, 0)
            settle(*forward())

        for rows, to in spots:
            for h in heads:
                dp = dot(vext[rows], doz[h], NT) - inn[0:1, h]
                x[to, h] = e[to, h] * dp.astype(BF16)

        outs = []
        for h in range(2):
            acc = jnp.zeros((64, 256), F32)
            for rows, to in spots:
                acc = acc + dot(kt[h * 64 : h * 64 + 64, rows], x[to, heads[h]])
            outs.append(acc * (rls[0:1, heads[h]] * 0.125))
        dq[at] = jnp.concatenate(outs, 0).T.astype(BF16)

        for rows, to in spots:
            acck[rows] = acck[rows] + dot(x[to], qs[...])
            accv[rows] = accv[rows] + dot(e[to], dos[...])
        return carry

    lax.fori_loop(0, 4, block_step, 0, unroll=2)

    b1, b2, b3 = BASE[1:]
    for which, acc, own in ((0, acck, gk), (1, accv, gv)):
        low, up = side.at[0, which], side.at[1, which]
        own[...] = acc[256:1280]
        for i, row in enumerate((640, 512, 384, 256)):
            spread_rows(own, i * 256, acc[b1 + row : b1 + row + 128], 2)
        gtmp[0:256] = acc[0:256]
        spread_rows(gtmp, 0, acc[b1 : b1 + 128], 2)
        spread_rows(gtmp, 0, acc[b2 + 448 : b2 + 512], 4)
        gtmp[256:384] = acc[b1 + 128 : b1 + 256]
        spread_rows(gtmp, 256, acc[b2 + 384 : b2 + 448], 2)
        gtmp[384:640] = acc[1280:1536]
        spread_rows(gtmp, 384, acc[b1 + 896 : b1 + 1024], 2)
        spread_rows(gtmp, 384, acc[b2 : b2 + 64], 4)
        gtmp[640:768] = acc[b1 + 768 : b1 + 896]
        spread_rows(gtmp, 640, acc[b2 + 64 : b2 + 128], 2)
        low[0:384] = gtmp[0:384].astype(BF16)
        up[0:384] = gtmp[384:768].astype(BF16)
        low[384:512] = acc[b2 + 128 : b2 + 256].astype(BF16)
        up[384:512] = acc[b2 + 256 : b2 + 384].astype(BF16)
        cross[which, 512:640] = acc[b3 : b3 + 128].astype(BF16)
        small[which] = acc[b3 + 128 : ROWS].astype(BF16)

        @pl.when(even)
        def _():
            rh[which] = up[...]
            rdown[which, 0:512] = low[...]
            rdown[which, 512:640] = cross[which, 512:640]
            rup[which, 0:256] = small[which]

        @pl.when(odd)
        def _():
            rh[which] = low[...]
            rup[which, 0:512] = up[...]
            rup[which, 512:640] = cross[which, 512:640]
            rdown[which, 0:256] = small[which]


def pass_on(role, token):
    token[0] = role[0]
    token[1] = role[1]


def add_down(ref, rows, own):
    add_rows(ref, 0, rows[0:256], 1)
    if own:
        add_rows(ref, 256, rows[256:384], 2)
        add_rows(ref, 512, rows[384:512], 4)
    else:
        add_rows(ref, 512, rows[256:384], 1)
        add_rows(ref, 640, rows[384:448], 2)
        add_rows(ref, 256, rows[448:512], 4)


def add_up(ref, rows, own):
    if own:
        add_rows(ref, 768, rows[0:256], 1)
        add_rows(ref, 512, rows[256:384], 2)
        add_rows(ref, 0, rows[384:512], 4)
    else:
        add_rows(ref, 256, rows[0:256], 1)
        add_rows(ref, 640, rows[256:384], 1)
        add_rows(ref, 0, rows[384:448], 4)
        add_rows(ref, 512, rows[448:512], 2)


def moved(array, pairs):
    return lax.ppermute(array, AXES, pairs)


def shape(*dims, dtype=BF16):
    return jax.ShapeDtypeStruct(dims, dtype)


def vmem(limit):
    return pltpu.CompilerParams(vmem_limit_bytes=limit * 2**20)


SMEM = pl.BlockSpec(memory_space=pltpu.SMEM)


def both(rows):
    return pl.BlockSpec((None, 2, rows, PAIR), lambda j: (j, 0, 0, 0))


def own_rows():
    return pl.BlockSpec((None, 1024, PAIR), lambda j: (j, 0, 0))


def columns(start):
    return pl.BlockSpec((1024, PAIR), lambda j: (0, start + j))


TOKEN = shape(2, dtype=jnp.int32)


def pair_rows(role, keys, values, start, pairs):
    def body(role, k, v, out, token, tmp):
        pass_on(role, token)
        for which, own in ((0, k), (1, v)):
            tmp[...] = own[256:768].astype(F32)
            out[which, 0:256] = own[0:256]
            out[which, 256:512] = own[768:1024]
            out[which, 512:768] = mean_rows(tmp, 0, 256, 2)

    return pl.pallas_call(
        body,
        grid=(pairs,),
        in_specs=[SMEM] + [columns(start)] * 2,
        out_specs=[both(768), SMEM],
        out_shape=[shape(pairs, 2, 768, PAIR), TOKEN],
        scratch_shapes=[pltpu.VMEM((512, PAIR), F32)],
        compiler_params=vmem(LIMIT),
        name="pair_rows",
    )(role, keys, values)


def cross_rows(role, keys, values, partner, start, pairs):
    def body(role, k, v, p, near, up_out, down_out, token, spans, tmp, ours):
        even, wrap = role[0] == 0, role[1]
        odd = jnp.logical_not(even)
        pass_on(role, token)

        for which, own in ((0, k), (1, v)):
            tmp[...] = p[which].astype(F32)
            ours[...] = own[...].astype(F32)
            spans[0:128] = mean_rows(ours, 0, 128, 8)
            spans[128:160] = mean_rows(tmp, 0, 32, 8)
            spans[160:192] = mean_rows(tmp, 512, 32, 4)
            spans[192:224] = mean_rows(tmp, 640, 32, 4)
            spans[224:256] = mean_rows(tmp, 256, 32, 8)

            def theirs_down(out):
                out[which, 0:256] = p[which, 0:256]
                out[which, 256:384] = p[which, 512:640]
                out[which, 384:448] = mean_rows(tmp, 640, 64, 2)
                out[which, 448:512] = mean_rows(tmp, 256, 64, 4)

            def theirs_up(out):
                out[which, 0:256] = p[which, 256:512]
                out[which, 256:384] = p[which, 640:768]
                out[which, 384:448] = mean_rows(tmp, 0, 64, 4)
                out[which, 448:512] = mean_rows(tmp, 512, 64, 2)

            @pl.when(even)
            def _():
                theirs_down(near)
                theirs_up(up_out)
                up_out[which, 512:640] = spans[0:128]
                down_out[which, 0:256] = spans[...]

            @pl.when(odd)
            def _():
                theirs_up(near)
                theirs_down(down_out)
                down_out[which, 512:640] = spans[0:128]
                up_out[which, 0:256] = spans[...]

            @pl.when((wrap == 1) & even)
            def _():
                down_out[which, 0:256] = own[0:256]
                down_out[which, 256:384] = mean_rows(ours, 256, 128, 2)
                down_out[which, 384:512] = mean_rows(ours, 512, 128, 4)
                down_out[which, 512:640] = spans[128:256]

            @pl.when((wrap == 1) & odd)
            def _():
                up_out[which, 0:256] = own[768:1024]
                up_out[which, 256:384] = mean_rows(ours, 512, 128, 2)
                up_out[which, 384:512] = mean_rows(ours, 0, 128, 4)
                up_out[which, 512:640] = spans[128:256]

            @pl.when((wrap == 2) & even)
            def _():
                up_out[which, 0:128] = spans[128:256]
                up_out[which, 128:256] = spans[0:128]

            @pl.when((wrap == 2) & odd)
            def _():
                down_out[which, 0:128] = spans[128:256]
                down_out[which, 128:256] = spans[0:128]

    return pl.pallas_call(
        body,
        grid=(pairs,),
        in_specs=[SMEM, columns(start), columns(start), both(768)],
        out_specs=[both(512), both(640), both(640), SMEM],
        out_shape=[shape(pairs, 2, rows, PAIR) for rows in (512, 640, 640)] + [TOKEN],
        scratch_shapes=[
            pltpu.VMEM((256, PAIR), BF16), pltpu.VMEM((768, PAIR), F32), pltpu.VMEM((1024, PAIR), F32),
        ],
        compiler_params=vmem(LIMIT),
        name="cross_rows",
    )(role, keys, values, partner)


def attend(role, valid, queries, keys, values, grad_out, came, before, start, pairs):

    def side(rows, which):
        return pl.BlockSpec((None, None, rows, PAIR), lambda j: (j, which, 0, 0))

    extra = 0 if before is None else 2

    def body(*refs):
        attend_kernel(*refs[:12], *refs[12 + extra :])

    heights = (512, 640, 640)
    whole = shape(1024, queries.shape[1])
    return pl.pallas_call(
        body,
        grid=(pairs,),
        in_specs=[SMEM, SMEM] + [columns(start)] * 4
        + [side(rows, which) for rows in heights for which in (0, 1)]
        + [pl.BlockSpec(memory_space=pl.ANY)] * extra,
        out_specs=[columns(start)] * 2 + [own_rows()] * 2 + [both(rows) for rows in heights]
        + [SMEM],
        out_shape=[whole, whole]
        + [shape(pairs, 1024, PAIR, dtype=F32)] * 2
        + [shape(pairs, 2, rows, PAIR) for rows in heights]
        + [TOKEN],
        input_output_aliases={12: 0, 13: 1} if extra else {},
        scratch_shapes=[
            pltpu.VMEM((ROWS, PAIR), BF16), pltpu.VMEM((ROWS, PAIR), BF16),
            pltpu.VMEM((PAIR, ROWS), BF16), pltpu.VMEM((2, 80, ROWS), BF16),
        ]
        + [pltpu.VMEM((1920, 512), BF16)] * 2
        + [pltpu.VMEM((512, PAIR), BF16)] * 4
        + [pltpu.VMEM((ROWS, PAIR), F32)] * 2
        + [pltpu.VMEM((8, 512), F32)] * 2
        + [
            pltpu.VMEM((1024, PAIR), F32), pltpu.VMEM((768, PAIR), F32),
            pltpu.VMEM((2, 640, PAIR), BF16), pltpu.VMEM((2, 256, PAIR), BF16),
            pltpu.VMEM((2, 2, 512, PAIR), BF16),
            pltpu.SMEM((1,), jnp.int32), pltpu.SMEM((ROWS // 128,), F32),
        ],
        compiler_params=vmem(LIMIT),
        cost_estimate=pl.CostEstimate(
            flops=pairs * 14 * 10**9, bytes_accessed=pairs * 4 * 10**6, transcendentals=0
        ),
        name="attend_pairs",
    )(
        role, valid, queries, keys, values, grad_out,
        *[part for pair in came for part in (pair, pair)], *(before or ()),
    )


def pair_grads(role, near, above, below, pairs):
    def body(role, near, above, below, out, token, tmp):
        even, wrap = role[0] == 0, role[1]
        odd = jnp.logical_not(even)
        pass_on(role, token)

        def add_span(rows):
            add_rows(tmp, 0, rows[0:32], 8)
            add_rows(tmp, 512, rows[32:64], 4)
            add_rows(tmp, 640, rows[64:96], 4)
            add_rows(tmp, 256, rows[96:128], 8)

        for which in (0, 1):
            tmp[...] = jnp.zeros_like(tmp)

            @pl.when(even)
            def _():
                add_down(tmp, near[which], False)

                @pl.when(wrap != 2)
                def _():
                    add_up(tmp, above[which, 0:512], False)

                @pl.when(wrap == 2)
                def _():
                    add_span(above[which, 0:128])

                @pl.when(wrap == 1)
                def _():
                    add_span(below[which, 512:640])

                @pl.when(wrap != 1)
                def _():
                    add_span(below[which, 128:256])

            @pl.when(odd)
            def _():
                add_up(tmp, near[which], False)

                @pl.when(wrap != 2)
                def _():
                    add_down(tmp, below[which, 0:512], False)

                @pl.when(wrap == 2)
                def _():
                    add_span(below[which, 0:128])

                @pl.when(wrap == 1)
                def _():
                    add_span(above[which, 512:640])

                @pl.when(wrap != 1)
                def _():
                    add_span(above[which, 128:256])

            out[which] = tmp[...].astype(BF16)

    return pl.pallas_call(
        body,
        grid=(pairs,),
        in_specs=[SMEM, both(512), both(640), both(640)],
        out_specs=[both(768), SMEM],
        out_shape=[shape(pairs, 2, 768, PAIR), TOKEN],
        scratch_shapes=[pltpu.VMEM((768, PAIR), F32)],
        compiler_params=vmem(LIMIT),
        name="pair_grads",
    )(role, near, above, below)


def finish(role, own_k, own_v, above, below, partner, before, start, pairs):
    extra = 0 if before is None else 2

    def body(*refs):
        role, gk, gv, above, below, got = refs[:6]
        dk, dv, token, tmp = refs[6 + extra :]
        even, wrap = role[0] == 0, role[1]
        odd = jnp.logical_not(even)
        pass_on(role, token)
        for which, own, out in ((0, gk, dk), (1, gv, dv)):
            tmp[...] = own[...]
            add_rows(tmp, 0, got[which, 0:256], 1)
            add_rows(tmp, 768, got[which, 256:512], 1)
            add_rows(tmp, 256, got[which, 512:768], 2)

            for here, large, small, add in ((even, above, below, add_down), (odd, below, above, add_up)):

                @pl.when(here & (wrap != 2))
                def _():
                    add_rows(tmp, 0, large[which, 512:640], 8)

                @pl.when(here & (wrap == 2))
                def _():
                    add_rows(tmp, 0, large[which, 128:256], 8)

                @pl.when(here & (wrap != 1))
                def _():
                    add_rows(tmp, 0, small[which, 0:128], 8)

                @pl.when(here & (wrap == 1))
                def _():
                    add(tmp, small[which, 0:512], True)

            out[...] = tmp[...].astype(BF16)

    whole = shape(1024, 1024)
    return pl.pallas_call(
        body,
        grid=(pairs,),
        in_specs=[SMEM] + [own_rows()] * 2 + [both(640), both(640), both(768)]
        + [pl.BlockSpec(memory_space=pl.ANY)] * extra,
        out_specs=[columns(start)] * 2 + [SMEM],
        out_shape=[whole, whole, TOKEN],
        input_output_aliases={6: 0, 7: 1} if extra else {},
        scratch_shapes=[pltpu.VMEM((1024, PAIR), F32)],
        compiler_params=vmem(LIMIT),
        name="sum_grads",
    )(role, own_k, own_v, above, below, partner, *(before or ()))


def routes(outer, inner):
    count = outer * inner
    up = {i: i + 2 for i in range(count - 2)}
    for a in range(1, outer - 1, 2):
        last = a * inner + inner - 2
        up[last], up[last + 1] = last + 3, last + 2
    return [(i, i ^ 1) for i in range(count)], sorted(up.items())


def local(queries, keys, values, grad_out):
    a, b = lax.axis_index(AXES[0]), lax.axis_index(AXES[1])
    outer, inner = lax.axis_size(AXES[0]), lax.axis_size(AXES[1])
    index = a * inner + b
    count = outer * inner
    partners, up = routes(outer, inner)
    down = [(j, i) for i, j in up]
    above = (a % 2 == 1) & (a < outer - 1) & (b >= inner - 2)
    below = (a % 2 == 0) & (a > 0) & (b < 2)
    ends = (b == 0) | (b == inner - 1)
    odd = index % 2
    wrap = jnp.where(above | below, jnp.where(ends, 1, 2), 0)
    token = jnp.stack([odd, wrap]).astype(jnp.int32)
    sign = 1 - 2 * odd

    def there(step):
        at = index + step * sign
        return (at >= 0) & (at < count)

    valid = jnp.stack(
        [index > 0, index < count - 1, there(-2), there(2), there(3)]
    ).astype(F32)

    starts = [sum(GROUPS[:i]) for i in range(len(GROUPS))]
    partner, came, grown, near, answers, returned = {}, {}, {}, {}, {}, {}
    mixed = grads = None
    for step, i in ORDER:
        start, pairs = starts[i], GROUPS[i]
        if step == "pair":
            rows, token = pair_rows(token, keys, values, start, pairs)
            partner[i] = moved(rows, partners)
        elif step == "cross":
            side, upward, downward, token = cross_rows(
                token, keys, values, partner[i], start, pairs
            )
            came[i] = (side, moved(upward, up), moved(downward, down))
        elif step == "attend":
            *mixed, gk, gv, near[i], upward, downward, token = attend(
                token, valid, queries, keys, values, grad_out, came[i], mixed, start, pairs
            )
            grown[i] = (gk, gv)
            answers[i] = (moved(downward, down), moved(upward, up))
        elif step == "back":
            rows, token = pair_grads(token, near[i], *answers[i], pairs)
            returned[i] = moved(rows, partners)
        else:
            *grads, token = finish(token, *grown[i], *answers[i], returned[i], grads, start, pairs)
    return (*mixed, *grads)


def solution(mesh):
    placed = P(AXES, None)
    return jax.shard_map(
        local,
        mesh=mesh,
        in_specs=(placed,) * 4,
        out_specs=(placed,) * 4,
        check_vma=False,
    )
```
